512 devices in a mesh: row: 16 (over x, z_lo), col: 32 (over z_hi, y, core).
Axes of the slice: x: 4, y: 4, z: 16 (z_hi: 4, z_lo: 4; z = z_hi * 4 + z_lo), core: 2. Of those that a mesh axis runs over, the one named last changes fastest.
Arguments:
- grad_out: bfloat16 [2048, 8192], P('col', 'row'), may hold values from -6 to 6
- gate_act: bfloat16 [2048, 28672], P('row', 'col'), may hold values from -6 to 6
- up_act: bfloat16 [2048, 28672], P('row', 'col'), may hold values from -6 to 6
- down_weight: bfloat16 [28672, 8192], P('col', 'row'), may hold values from -0.0625 to 0.0625
- counts: int32 [16], P('row'), may hold values from 32 to 128, as said below
- down_seed: int32 [1], replicated, may hold values from 0 to 1073741823
- up_seed: int32 [1], replicated, may hold values from 0 to 1073741823
Outputs:
- gate_grad: bfloat16 [2048, 28672], P('row', 'col')
- up_grad: bfloat16 [2048, 28672], P('row', 'col')
- features: float32 [16, 64, 64], P('row', 'col')
The draws below stay inside these ranges and needn't reach their ends.
Inputs may be any that keep to these rules, and one draw needn't show every extreme that they name: counts[e] is how many leading positions of example e carry tokens; some example has all 128 positions in every draw.
All inputs are finite; a program needn't handle non-finite values.
Results may differ from the reference program's by a relative error of at most 0.0027.
Values may be sent and summed in bfloat16 or wider, within the bound.
A program may use at most 64 MiB of HBM per device.

```python
import math
import jax
import jax.numpy as jnp
from jax import lax

D = 8192
FF = 28672
RANK = 64
SEQ_LEN = 128
EXAMPLES = 16
TOKENS = 2048
N_ROW = 16


def draw_counts(key, part):
    key = jax.random.fold_in(key, 7)
    key_values, key_choice = jax.random.split(key)
    values = jax.random.randint(key_values, (EXAMPLES,), SEQ_LEN // 4, SEQ_LEN + 1, dtype=jnp.int32)
    chosen = jax.random.randint(key_choice, (), 0, EXAMPLES, dtype=jnp.int32)
    return jnp.where(jnp.arange(EXAMPLES, dtype=jnp.int32) == chosen, SEQ_LEN, values).astype(jnp.int32)


def raised(entries, rng, source, target, shards_of, factor):
    def block_of(axis_at):
        return (jnp.arange(entries.shape[axis_at]) // (entries.shape[axis_at] // shards_of)).reshape((-1,) + (1,) * (entries.ndim - 1 - axis_at))

    near = jax.random.permutation(rng, shards_of)[block_of(target)]
    far = (block_of(target) + shards_of // 2) % shards_of
    return jnp.where((block_of(source) == near) | (block_of(source) == far), factor * entries, entries)


def block_scale(key, shape, cuts, least, largest):
    def one(axis_at, shards_of):
        heights = jax.random.uniform(jax.random.fold_in(jax.random.fold_in(key, 6), axis_at), (shards_of,), jnp.float32, least / len(cuts), largest / len(cuts))
        return jnp.repeat(jnp.exp(heights), shape[axis_at] // shards_of).reshape((-1,) + (1,) * (len(shape) - axis_at - 1))

    factor_of = one(*cuts[0])
    for cut in cuts[1:]:
        factor_of = factor_of * one(*cut)
    return factor_of


def scatter_about(key, dims, spread, reach, cuts=(), held_as=jnp.bfloat16):
    gain = block_scale(key, dims, cuts, -0.22, 0.18) if cuts else 1.0
    entries = jax.random.normal(key, dims, jnp.float32) * spread * gain
    return jnp.minimum(jnp.maximum(entries, -reach), reach).astype(held_as)


def heavy_noise(own_key, shape, deviation, most, shards, heavy, held_as=jnp.bfloat16):
    drawn = deviation * jax.random.normal(own_key, shape, jnp.float32)
    if shards:
        drawn = drawn * block_scale(own_key, shape, shards, -0.22, 0.18)
    return jnp.clip(raised(drawn, jax.random.fold_in(own_key, 3), *heavy), -most, most).astype(held_as)


def setup_inputs(seed: int = 0) -> dict:
    splits = jax.random.split(jax.random.key(seed), 8)
    return {
        "grad_out": heavy_noise(splits[0], (TOKENS, D), 1.0, 6.0, ((0, 32), (1, 16)), (1, 0, 32, 2.75)),
        "gate_act": scatter_about(splits[1], (TOKENS, FF), 1.0, 6.0, ((0, 16), (1, 32))),
        "up_act": scatter_about(splits[2], (TOKENS, FF), 1.0, 6.0, ((0, 16), (1, 32))),
        "down_weight": scatter_about(splits[3], (FF, D), D ** -0.5, 0.0625, ((0, 32), (1, 16))),
        "counts": draw_counts(jax.random.fold_in(splits[7], 71), 0),
        "down_seed": jax.random.randint(splits[5], (1,), 0, 1073741824).astype(jnp.int32),
        "up_seed": jax.random.randint(splits[6], (1,), 0, 1073741824).astype(jnp.int32),
    }


def scramble(values):
    values = values ^ values >> 16 & 65535
    values = values * 73244475
    values = values ^ values >> 16 & 65535
    values = values * 73244475
    return values ^ values >> 16 & 65535

def projection(seed_value, first_row, row_count, rank_size):
    row_number = first_row + lax.broadcasted_iota(jnp.int32, (row_count, rank_size), 0)
    rank_number = lax.broadcasted_iota(jnp.int32, (row_count, rank_size), 1)
    seed_mix = scramble(seed_value + 40503)
    hashed = scramble(row_number * rank_size + rank_number ^ seed_mix)
    return ((hashed >> 8 & 255).astype(jnp.float32) - 127.5).astype(jnp.bfloat16)

def reference(grad_out, gate_act, up_act, down_weight, counts, down_seed, up_seed):
    block_width = D // N_ROW

    def add_block(totals, block_index):
        first_col = (block_index * block_width).astype(jnp.int32)
        grad_block = lax.dynamic_slice_in_dim(grad_out, first_col, block_width, 1)
        weight_block = lax.dynamic_slice_in_dim(down_weight, first_col, block_width, 1)
        up_block = projection(up_seed, first_col, block_width, RANK)
        hidden_term = lax.dot_general(grad_block, weight_block, (((1,), (1,)), ((), ())), preferred_element_type=jnp.float32)
        rank_term = jnp.dot(grad_block, up_block, preferred_element_type=jnp.float32)
        return ((totals[0] + hidden_term, totals[1] + rank_term), None)
    start_sums = (jnp.zeros((TOKENS, FF), jnp.float32), jnp.zeros((TOKENS, RANK), jnp.float32))
    (hidden_grad, rank_sum), ignored = lax.scan(add_block, start_sums, jnp.arange(N_ROW, dtype=jnp.int32))
    gate_value = gate_act.astype(jnp.float32)
    up_value = up_act.astype(jnp.float32)
    sigmoid_gate = jax.nn.sigmoid(gate_value)
    silu_gate = gate_value * sigmoid_gate
    gate_grad = (hidden_grad * up_value * sigmoid_gate * (1.0 + gate_value * (1.0 - sigmoid_gate))).astype(jnp.bfloat16)
    up_grad = (hidden_grad * silu_gate).astype(jnp.bfloat16)
    hidden = (silu_gate * up_value).astype(jnp.bfloat16)
    down_proj = projection(down_seed, 0, FF, RANK)
    hidden_ranks = jnp.dot(hidden, down_proj, preferred_element_type=jnp.float32) * (1.0 / math.sqrt(FF * 5461.25))
    grad_ranks = rank_sum * (1.0 / math.sqrt(D * 5461.25))
    positions = lax.broadcasted_iota(jnp.int32, (EXAMPLES, SEQ_LEN), 1)
    live_mask = jnp.where(positions < counts[:, None], 1.0, 0.0).astype(jnp.float32)
    masked = hidden_ranks.reshape(EXAMPLES, SEQ_LEN, RANK) * live_mask[:, :, None]
    features = jnp.einsum('etr,ets->ers', masked, grad_ranks.reshape(EXAMPLES, SEQ_LEN, RANK), precision=lax.Precision.HIGHEST)
    features = features * lax.rsqrt(counts.astype(jnp.float32))[:, None, None]
    return (gate_grad, up_grad, features)
```

```python
import math

import jax
import jax.numpy as jnp
from jax import lax
from jax.experimental import pallas as pl
from jax.experimental.pallas import tpu as pltpu
from jax.sharding import PartitionSpec as P

D = 8192
FF = 28672
RANK = 64
TOK = 128
PIECE = 64
WIDTH = 512
HID = 896
CHUNKS = ((0, 2), (2, 2), (4, 2), (6, 1))
NT = (((1,), (1,)), ((), ()))
MESH = pl.DeviceIdType.MESH
COPIES = 96


def scramble(values):
    values = values ^ values >> 16 & 65535
    values = values * 73244475
    values = values ^ values >> 16 & 65535
    values = values * 73244475
    return values ^ values >> 16 & 65535


def projection_t(seed_value, first_row, row_count):
    row_number = first_row + lax.broadcasted_iota(jnp.int32, (RANK, row_count), 1)
    rank_number = lax.broadcasted_iota(jnp.int32, (RANK, row_count), 0)
    seed_mix = scramble(seed_value + 40503)
    hashed = scramble(row_number * RANK + rank_number ^ seed_mix)
    return ((hashed >> 8 & 255).astype(jnp.float32) - 127.5).astype(jnp.bfloat16)


def kernel(
    grad_ref, gate_ref, up_ref, weight_ref, counts_ref, down_seed_ref, up_seed_ref,
    gate_out, up_out, feat_out,
    gate_in, up_in, weights, zblocks, grads, up_proj, down_proj, hidden,
    gate_factor, up_factor, own, partial, part_out, part_in, rank_out, rank_in,
    feat_z, feat_z_in, feat_y, feat_y_in, feat_c, feat_c_in,
    send_sem, recv_sem, local_sem, cross_send, cross_recv,
):
    row = lax.axis_index("row")
    col = lax.axis_index("col")
    x, zl = lax.div(row, 4), lax.rem(row, 4)
    zh, y, c = lax.div(col, 8), lax.rem(lax.div(col, 2), 4), lax.rem(col, 2)

    def turn(value, step):
        return lax.rem(value + step, 4)

    def device(x=x, zl=zl, zh=zh, y=y, c=c):
        return (x * 4 + zl, (zh * 4 + y) * 2 + c)

    sibling = device(c=1 - c)
    started = []

    def send(src, dst, target):
        index = len(started)
        copy = pltpu.make_async_remote_copy(
            src_ref=src, dst_ref=dst, send_sem=send_sem.at[index], recv_sem=recv_sem.at[index],
            device_id=target, device_id_type=MESH,
        )
        copy.start()
        started.append(copy)
        return copy

    locals_ = []
    for number, (src, dst) in enumerate(
        ((weight_ref, weights.at[x]), (gate_ref, gate_in), (up_ref, up_in))
    ):
        copy = pltpu.make_async_copy(src, dst, local_sem.at[number])
        copy.start()
        locals_.append(copy)

    barrier = pltpu.get_barrier_semaphore()
    peers = [sibling]
    for step in (1, 2, 3):
        peers += [
            device(x=turn(x, step)), device(zl=turn(zl, step)),
            device(zh=turn(zh, step)), device(y=turn(y, step)),
        ]
    for peer in peers:
        pl.semaphore_signal(barrier, inc=1, device_id=peer, device_id_type=MESH)
    pl.semaphore_wait(barrier, len(peers))


    def mine(group):
        return pl.ds(pl.multiple_of(group * TOK + c * PIECE, PIECE), PIECE)

    def cross(step, src):
        target = turn(zh, step)
        slot = grads.at[x, mine(y)]
        remote = pltpu.make_async_remote_copy(
            src_ref=src, dst_ref=slot, send_sem=cross_send.at[step], recv_sem=cross_recv.at[x],
            device_id=device(x=target), device_id_type=MESH,
        )
        local = pltpu.make_async_copy(src, slot, local_sem.at[3])

        @pl.when(target != x)
        def _():
            remote.start()

        @pl.when(target == x)
        def _():
            local.start()

        return target, remote

    def send_weight(chunk):
        first, count = CHUNKS[chunk]
        rows = pl.ds(first * 128, count * 128)
        right = send(weight_ref.at[rows], weights.at[x, rows], device(x=turn(x, 1)))
        left = send(weight_ref.at[rows], weights.at[x, rows], device(x=turn(x, 3)))
        return right, left

    def forward_weight(chunk, copies):
        first, count = CHUNKS[chunk]
        right, left = copies
        half = count * 64
        right.wait_recv()
        rows = pl.ds(first * 128, half)
        block = weights.at[turn(x, 3), rows]
        on_right = send(block, block, device(x=turn(x, 1)))
        left.wait_recv()
        rows = pl.ds(first * 128 + half, half)
        block = weights.at[turn(x, 1), rows]
        on_left = send(block, block, device(x=turn(x, 3)))
        return on_right, on_left

    z_up = send(grad_ref, zblocks.at[zh], device(zh=turn(zh, 1)))
    z_down = send(grad_ref, zblocks.at[zh], device(zh=turn(zh, 3)))
    crossed = [cross(0, grad_ref)]
    w0 = send_weight(0)
    w1 = send_weight(1)

    down_proj[...] = projection_t(down_seed_ref[0], col * HID, HID)
    for part in range(4):
        up_proj[part] = projection_t(up_seed_ref[0], (part * 4 + zl) * WIDTH, WIDTH)
    locals_[1].wait()
    locals_[2].wait()
    for part in range(7):
        cols = slice(part * 128, part * 128 + 128)
        gate_value = gate_in[:, cols].astype(jnp.float32)
        up_value = up_in[:, cols].astype(jnp.float32)
        sigmoid_gate = jax.nn.sigmoid(gate_value)
        silu_gate = gate_value * sigmoid_gate
        gate_factor[:, cols] = up_value * sigmoid_gate * (1.0 + gate_value * (1.0 - sigmoid_gate))
        up_factor[:, cols] = silu_gate
        hidden[:, cols] = (silu_gate * up_value).astype(jnp.bfloat16)

    z_up.wait_recv()
    block = zblocks.at[turn(zh, 3), pl.ds(0, 32)]
    z_on_up = send(block, block, device(zh=turn(zh, 1)))
    crossed.append(cross(3, zblocks.at[turn(zh, 3)]))
    z_down.wait_recv()
    block = zblocks.at[turn(zh, 1), pl.ds(32, 32)]
    z_on_down = send(block, block, device(zh=turn(zh, 3)))
    crossed.append(cross(1, zblocks.at[turn(zh, 1)]))

    w0_on = forward_weight(0, w0)
    w2 = send_weight(2)
    hidden_ranks = lax.dot_general(
        down_proj[...], hidden[...], NT, preferred_element_type=jnp.float32
    ) * (1.0 / math.sqrt(FF * 5461.25))

    z_on_up.wait_recv()
    z_on_down.wait_recv()
    crossed.append(cross(2, zblocks.at[turn(zh, 2)]))
    w3 = send_weight(3)

    pltpu.make_async_copy(grad_ref, grads.at[x, mine(y)], local_sem.at[3]).wait()
    for step in (1, 2, 3):
        source = turn(x, step)
        slot = grads.at[source, mine(y)]
        pltpu.make_async_remote_copy(
            src_ref=slot, dst_ref=slot, send_sem=cross_send.at[step], recv_sem=cross_recv.at[source],
            device_id=device(x=source), device_id_type=MESH,
        ).wait_recv()

    def y_block(source, first=0, count=4):
        return grads.at[pl.ds(first, count), mine(source)]

    block = y_block(y)
    y_up = send(block, block, device(y=turn(y, 1)))
    y_down = send(block, block, device(y=turn(y, 3)))
    across = [send(block, block, sibling)]
    w1_on = forward_weight(1, w1)

    y_up.wait_recv()
    block = y_block(turn(y, 3), 0, 2)
    y_on_up = send(block, block, device(y=turn(y, 1)))
    block = y_block(turn(y, 3))
    across.append(send(block, block, sibling))
    y_down.wait_recv()
    block = y_block(turn(y, 1), 2, 2)
    y_on_down = send(block, block, device(y=turn(y, 3)))
    block = y_block(turn(y, 1))
    across.append(send(block, block, sibling))
    w2_on = forward_weight(2, w2)
    w3_on = forward_weight(3, w3)
    y_on_up.wait_recv()
    block = y_block(turn(y, 2), 0, 2)
    across.append(send(block, block, sibling))
    y_on_down.wait_recv()
    block = y_block(turn(y, 2), 2, 2)
    across.append(send(block, block, sibling))
    for copy in across:
        copy.wait_recv()

    rank_copies = []
    rank_own = None
    for step in (1, 2, 3, 0):
        target = turn(zl, step)
        rows = pl.ds(pl.multiple_of(target * TOK, TOK), TOK)
        total = jnp.zeros((RANK, TOK), jnp.float32)
        for part in range(4):
            total += lax.dot_general(
                up_proj[part], grads[part, rows], NT, preferred_element_type=jnp.float32
            )
        if step:
            rank_out[step - 1] = total
            rank_copies.append(send(rank_out.at[step - 1], rank_in.at[step - 1], device(zl=target)))
        else:
            rank_own = total

    def multiply(chunk):
        first, count = CHUNKS[chunk]
        rows = pl.ds(first * 128, count * 128)
        copies = []
        lanes = slice(0, count * 128)
        for part in range(4):
            product = lax.dot_general(
                grads[part], weights[part, rows], NT, preferred_element_type=jnp.float32
            )
            partial[:, lanes] = product if part == 0 else partial[:, lanes] + product
        for step in (2, 3, 1, 0):
            target = turn(zl, step)
            tokens = pl.ds(pl.multiple_of(target * TOK, TOK), TOK)
            if step:
                for lane in range(count):
                    part_out[step - 1, first + lane] = partial[
                        tokens, lane * 128 : lane * 128 + 128
                    ].astype(jnp.bfloat16)
                blocks = pl.ds(first, count)
                copies.append(
                    send(
                        part_out.at[step - 1, blocks], part_in.at[step - 1, blocks],
                        device(zl=target),
                    )
                )
            else:
                own[:, rows] = partial[tokens, lanes]
        return copies

    def finish(chunk, copies):
        first, count = CHUNKS[chunk]
        for copy in copies:
            copy.wait_recv()
        for lane in range(first, first + count):
            cols = slice(lane * 128, lane * 128 + 128)
            total = own[:, cols]
            for source in range(3):
                total += part_in[source, lane].astype(jnp.float32)
            gate_out[:, cols] = (total * gate_factor[:, cols]).astype(jnp.bfloat16)
            up_out[:, cols] = (total * up_factor[:, cols]).astype(jnp.bfloat16)

    locals_[0].wait()
    parts = []
    for chunk, copies in ((0, w0_on), (1, w1_on)):
        for copy in copies:
            copy.wait_recv()
        parts.append(multiply(chunk))

    for copy in rank_copies:
        copy.wait_recv()
    grad_ranks = (rank_own + rank_in[0] + rank_in[1] + rank_in[2]) * (
        1.0 / math.sqrt(D * 5461.25)
    )
    live_count = counts_ref[0]
    positions = lax.broadcasted_iota(jnp.int32, (RANK, TOK), 1)
    masked = hidden_ranks * jnp.where(positions < live_count, 1.0, 0.0)
    features = lax.dot_general(
        masked, grad_ranks, NT, precision=lax.Precision.HIGHEST, preferred_element_type=jnp.float32
    )
    feat_z[...] = jnp.zeros_like(feat_z)
    for owner in range(32):
        feat_z[owner, 0:2, 0:RANK] = features[owner * 2 : owner * 2 + 2, :]
    z_copies = [
        send(
            feat_z.at[pl.ds(turn(zh, step) * 8, 8)], feat_z_in.at[step - 1],
            device(zh=turn(zh, step)),
        )
        for step in (1, 2, 3)
    ]

    for copy in w2_on:
        copy.wait_recv()
    parts.append(multiply(2))

    for copy in z_copies:
        copy.wait_recv()
    feat_y[...] = feat_z[pl.ds(zh * 8, 8)] + feat_z_in[0] + feat_z_in[1] + feat_z_in[2]
    y_copies = [
        send(
            feat_y.at[pl.ds(turn(y, step) * 2, 2)], feat_y_in.at[step - 1],
            device(y=turn(y, step)),
        )
        for step in (1, 2, 3)
    ]

    for copy in w3_on:
        copy.wait_recv()
    parts.append(multiply(3))

    for copy in y_copies:
        copy.wait_recv()
    feat_c[...] = feat_y[pl.ds(y * 2, 2)] + feat_y_in[0] + feat_y_in[1] + feat_y_in[2]
    c_copy = send(feat_c.at[1 - c], feat_c_in, sibling)

    for chunk in (0, 1, 2):
        finish(chunk, parts[chunk])
    c_copy.wait_recv()
    counted = jnp.full((8, 128), live_count, jnp.int32).astype(jnp.float32)
    result = (feat_c[c] + feat_c_in[...]) * lax.rsqrt(counted)
    feat_out[0] = result[0:2, 0:RANK]
    finish(3, parts[3])

    for copy in started:
        copy.wait_send()
    for target, remote in crossed:

        @pl.when(target != x)
        def _(remote=remote):
            remote.wait_send()


def shards(grad_out, gate_act, up_act, down_weight, counts, down_seed, up_seed):
    hbm = pl.BlockSpec(memory_space=pltpu.HBM)
    smem = pl.BlockSpec(memory_space=pltpu.SMEM)
    vmem = pl.BlockSpec(memory_space=pltpu.VMEM)
    bf16, f32 = jnp.bfloat16, jnp.float32
    return pl.pallas_call(
        kernel,
        out_shape=(
            jax.ShapeDtypeStruct((TOK, HID), bf16),
            jax.ShapeDtypeStruct((TOK, HID), bf16),
            jax.ShapeDtypeStruct((1, 2, RANK), f32),
        ),
        in_specs=[hbm, hbm, hbm, hbm, smem, smem, smem],
        out_specs=(vmem, vmem, vmem),
        scratch_shapes=[
            pltpu.VMEM((TOK, HID), bf16),
            pltpu.VMEM((TOK, HID), bf16),
            pltpu.VMEM((4, HID, WIDTH), bf16),
            pltpu.VMEM((4, PIECE, WIDTH), bf16),
            pltpu.VMEM((4, 4 * TOK, WIDTH), bf16),
            pltpu.VMEM((4, RANK, WIDTH), bf16),
            pltpu.VMEM((RANK, HID), bf16),
            pltpu.VMEM((TOK, HID), bf16),
            pltpu.VMEM((TOK, HID), f32),
            pltpu.VMEM((TOK, HID), f32),
            pltpu.VMEM((TOK, HID), f32),
            pltpu.VMEM((4 * TOK, 256), f32),
            pltpu.VMEM((3, 7, TOK, 128), bf16),
            pltpu.VMEM((3, 7, TOK, 128), bf16),
            pltpu.VMEM((3, RANK, TOK), f32),
            pltpu.VMEM((3, RANK, TOK), f32),
            pltpu.VMEM((32, 8, 128), f32),
            pltpu.VMEM((3, 8, 8, 128), f32),
            pltpu.VMEM((8, 8, 128), f32),
            pltpu.VMEM((3, 2, 8, 128), f32),
            pltpu.VMEM((2, 8, 128), f32),
            pltpu.VMEM((8, 128), f32),
            pltpu.SemaphoreType.DMA((COPIES,)),
            pltpu.SemaphoreType.DMA((COPIES,)),
            pltpu.SemaphoreType.DMA((4,)),
            pltpu.SemaphoreType.DMA((4,)),
            pltpu.SemaphoreType.DMA((4,)),
        ],
        compiler_params=pltpu.CompilerParams(
            collective_id=0, has_side_effects=True, vmem_limit_bytes=60 * 1024 * 1024
        ),
    )(grad_out, gate_act, up_act, down_weight, counts, down_seed, up_seed)


def solution(mesh):
    in_specs = (
        P("col", "row"),
        P("row", "col"),
        P("row", "col"),
        P("col", "row"),
        P("row"),
        P(),
        P(),
    )
    out_specs = (P("row", "col"), P("row", "col"), P("row", "col", None))
    return jax.shard_map(shards, mesh=mesh, in_specs=in_specs, out_specs=out_specs, check_vma=False)
```

```python
import math

import jax
import jax.numpy as jnp
from jax import lax
from jax.experimental import pallas as pl
from jax.experimental.pallas import tpu as pltpu
from jax.sharding import PartitionSpec as P

D = 8192
FF = 28672
RANK = 64
TOK = 128
PIECE = 64
WIDTH = 512
HID = 896
CHUNKS = ((0, 2), (2, 2), (4, 2), (6, 1))
NT = (((1,), (1,)), ((), ()))
MESH = pl.DeviceIdType.MESH
COPIES = 96


def scramble(values):
    values = values ^ values >> 16 & 65535
    values = values * 73244475
    values = values ^ values >> 16 & 65535
    values = values * 73244475
    return values ^ values >> 16 & 65535


def projection_t(seed_value, first_row, row_count):
    row_number = first_row + lax.broadcasted_iota(jnp.int32, (RANK, row_count), 1)
    rank_number = lax.broadcasted_iota(jnp.int32, (RANK, row_count), 0)
    seed_mix = scramble(seed_value + 40503)
    hashed = scramble(row_number * RANK + rank_number ^ seed_mix)
    return ((hashed >> 8 & 255).astype(jnp.float32) - 127.5).astype(jnp.bfloat16)


def kernel(
    grad_ref, gate_ref, up_ref, weight_ref, counts_ref, down_seed_ref, up_seed_ref,
    gate_out, up_out, feat_out,
    gate_in, up_in, weights, zblocks, grads, up_proj, down_proj, hidden,
    gate_factor, up_factor, own, part_out, part_in, rank_own, rank_out, rank_in,
    feat_y, feat_y_in, feat_z, feat_z_in, feat_c, feat_c_in,
    send_sem, recv_sem, local_sem, cross_send, cross_recv, part_send, part_recv,
):
    row = lax.axis_index("row")
    col = lax.axis_index("col")
    x, zl = lax.div(row, 4), lax.rem(row, 4)
    zh, y, c = lax.div(col, 8), lax.rem(lax.div(col, 2), 4), lax.rem(col, 2)

    def turn(value, step):
        return lax.rem(value + step, 4)

    def device(x=x, zl=zl, zh=zh, y=y, c=c):
        return (x * 4 + zl, (zh * 4 + y) * 2 + c)

    sibling = device(c=1 - c)
    started = []

    def send(src, dst, target):
        index = len(started)
        copy = pltpu.make_async_remote_copy(
            src_ref=src, dst_ref=dst, send_sem=send_sem.at[index], recv_sem=recv_sem.at[index],
            device_id=target, device_id_type=MESH,
        )
        copy.start()
        started.append(copy)
        return copy

    locals_ = []
    for number, (src, dst) in enumerate(
        ((weight_ref, weights.at[x]), (gate_ref, gate_in), (up_ref, up_in))
    ):
        copy = pltpu.make_async_copy(src, dst, local_sem.at[number])
        copy.start()
        locals_.append(copy)

    barrier = pltpu.get_barrier_semaphore()
    peers = [sibling]
    for step in (1, 2, 3):
        peers += [
            device(x=turn(x, step)), device(zl=turn(zl, step)),
            device(zh=turn(zh, step)), device(y=turn(y, step)),
        ]
    for peer in peers:
        pl.semaphore_signal(barrier, inc=1, device_id=peer, device_id_type=MESH)
    pl.semaphore_wait(barrier, len(peers))


    def mine(group):
        return pl.ds(pl.multiple_of(group * TOK + c * PIECE, PIECE), PIECE)

    def cross(step, src):
        target = turn(zh, step)
        slot = grads.at[x, mine(y)]
        remote = pltpu.make_async_remote_copy(
            src_ref=src, dst_ref=slot, send_sem=cross_send.at[step], recv_sem=cross_recv.at[x],
            device_id=device(x=target), device_id_type=MESH,
        )
        local = pltpu.make_async_copy(src, slot, local_sem.at[3])

        @pl.when(target != x)
        def _():
            remote.start()

        @pl.when(target == x)
        def _():
            local.start()

        return target, remote

    def send_weight(chunk):
        first, count = CHUNKS[chunk]
        rows = pl.ds(first * 128, count * 128)
        right = send(weight_ref.at[rows], weights.at[x, rows], device(x=turn(x, 1)))
        left = send(weight_ref.at[rows], weights.at[x, rows], device(x=turn(x, 3)))
        return right, left

    def forward_weight(chunk, copies):
        first, count = CHUNKS[chunk]
        right, left = copies
        half = count * 64
        right.wait_recv()
        rows = pl.ds(first * 128, half)
        block = weights.at[turn(x, 3), rows]
        on_right = send(block, block, device(x=turn(x, 1)))
        left.wait_recv()
        rows = pl.ds(first * 128 + half, half)
        block = weights.at[turn(x, 1), rows]
        on_left = send(block, block, device(x=turn(x, 3)))
        return on_right, on_left

    z_up = send(grad_ref, zblocks.at[zh], device(zh=turn(zh, 1)))
    z_down = send(grad_ref, zblocks.at[zh], device(zh=turn(zh, 3)))
    crossed = [cross(0, grad_ref)]
    w0 = send_weight(0)
    w1 = send_weight(1)

    down_proj[...] = projection_t(down_seed_ref[0], col * HID, HID)
    for part in range(4):
        up_proj[part] = projection_t(up_seed_ref[0], (part * 4 + zl) * WIDTH, WIDTH)
    locals_[1].wait()
    locals_[2].wait()
    for part in range(7):
        cols = slice(part * 128, part * 128 + 128)
        gate_value = gate_in[:, cols].astype(jnp.float32)
        up_value = up_in[:, cols].astype(jnp.float32)
        sigmoid_gate = jax.nn.sigmoid(gate_value)
        silu_gate = gate_value * sigmoid_gate
        gate_factor[:, cols] = up_value * sigmoid_gate * (1.0 + gate_value * (1.0 - sigmoid_gate))
        up_factor[:, cols] = silu_gate
        hidden[:, cols] = (silu_gate * up_value).astype(jnp.bfloat16)

    z_up.wait_recv()
    block = zblocks.at[turn(zh, 3), pl.ds(0, 32)]
    z_on_up = send(block, block, device(zh=turn(zh, 1)))
    crossed.append(cross(3, zblocks.at[turn(zh, 3)]))
    z_down.wait_recv()
    block = zblocks.at[turn(zh, 1), pl.ds(32, 32)]
    z_on_down = send(block, block, device(zh=turn(zh, 3)))
    crossed.append(cross(1, zblocks.at[turn(zh, 1)]))

    w0_on = forward_weight(0, w0)
    hidden_ranks = lax.dot_general(
        down_proj[...], hidden[...], NT, preferred_element_type=jnp.float32
    ) * (1.0 / math.sqrt(FF * 5461.25))

    z_on_up.wait_recv()
    z_on_down.wait_recv()
    crossed.append(cross(2, zblocks.at[turn(zh, 2)]))
    w2 = send_weight(2)

    pltpu.make_async_copy(grad_ref, grads.at[x, mine(y)], local_sem.at[3]).wait()
    for step in (1, 2, 3):
        source = turn(x, step)
        slot = grads.at[source, mine(y)]
        pltpu.make_async_remote_copy(
            src_ref=slot, dst_ref=slot, send_sem=cross_send.at[step], recv_sem=cross_recv.at[source],
            device_id=device(x=source), device_id_type=MESH,
        ).wait_recv()

    def y_block(source, first=0, count=4):
        return grads.at[pl.ds(first, count), mine(source)]

    def part_copy(chunk, step):
        target = turn(y, step)
        if chunk == 4:
            src, dst = rank_out.at[step], rank_in.at[zl]
        else:
            first, count = CHUNKS[chunk]
            src, dst = part_out.at[step, pl.ds(first, count)], part_in.at[zl, pl.ds(first, count)]
        return pltpu.make_async_remote_copy(
            src_ref=src, dst_ref=dst, send_sem=part_send.at[chunk * 4 + step],
            recv_sem=part_recv.at[chunk * 4 + zl], device_id=device(zl=target), device_id_type=MESH,
        )

    def wait_parts(chunk):
        for step in (1, 2, 3):
            source = turn(zl, step)
            if chunk == 4:
                block = rank_in.at[source]
            else:
                first, count = CHUNKS[chunk]
                block = part_in.at[source, pl.ds(first, count)]
            pltpu.make_async_remote_copy(
                src_ref=block, dst_ref=block, send_sem=part_send.at[chunk * 4 + step],
                recv_sem=part_recv.at[chunk * 4 + source], device_id=device(zl=source),
                device_id_type=MESH,
            ).wait_recv()

    def multiply(chunk, step):
        target = turn(y, step)
        tokens = pl.ds(pl.multiple_of(target * TOK, TOK), TOK)
        total = None
        for part in range(4):
            if chunk == 4:
                left, right = up_proj[part], grads[part, tokens]
            else:
                first, count = CHUNKS[chunk]
                rows = pl.ds(first * 128, count * 128)
                left, right = grads[part, tokens], weights[part, rows]
            product = lax.dot_general(left, right, NT, preferred_element_type=jnp.float32)
            total = product if part == 0 else total + product

        @pl.when(target == zl)
        def _():
            if chunk == 4:
                rank_own[...] = total
            else:
                own[:, rows] = total

        @pl.when(target != zl)
        def _():
            if chunk == 4:
                rank_out[step] = total
            else:
                for lane in range(count):
                    part_out[step, first + lane] = total[:, lane * 128 : lane * 128 + 128].astype(
                        jnp.bfloat16
                    )
            part_copy(chunk, step).start()

    def finish(chunk):
        wait_parts(chunk)
        first, count = CHUNKS[chunk]
        for lane in range(first, first + count):
            cols = slice(lane * 128, lane * 128 + 128)
            total = own[:, cols]
            for step in (1, 2, 3):
                total += part_in[turn(zl, step), lane].astype(jnp.float32)
            gate_out[:, cols] = (total * gate_factor[:, cols]).astype(jnp.bfloat16)
            up_out[:, cols] = (total * up_factor[:, cols]).astype(jnp.bfloat16)

    block = y_block(y)
    y_up = send(block, block, device(y=turn(y, 1)))
    y_down = send(block, block, device(y=turn(y, 3)))
    across = [send(block, block, sibling)]
    w1_on = forward_weight(1, w1)
    w3 = send_weight(3)

    locals_[0].wait()
    across[0].wait_recv()
    multiply(4, 0)
    for copy in w0_on:
        copy.wait_recv()
    multiply(0, 0)

    y_up.wait_recv()
    block = y_block(turn(y, 3), 0, 2)
    y_on_up = send(block, block, device(y=turn(y, 1)))
    block = y_block(turn(y, 3))
    across.append(send(block, block, sibling))
    y_down.wait_recv()
    block = y_block(turn(y, 1), 2, 2)
    y_on_down = send(block, block, device(y=turn(y, 3)))
    block = y_block(turn(y, 1))
    across.append(send(block, block, sibling))
    for copy in w1_on:
        copy.wait_recv()
    multiply(1, 0)

    across[1].wait_recv()
    multiply(4, 3)
    multiply(0, 3)
    w2_on = forward_weight(2, w2)
    across[2].wait_recv()
    multiply(4, 1)
    multiply(0, 1)
    y_on_up.wait_recv()
    block = y_block(turn(y, 2), 0, 2)
    across.append(send(block, block, sibling))
    y_on_down.wait_recv()
    block = y_block(turn(y, 2), 2, 2)
    across.append(send(block, block, sibling))
    multiply(1, 3)
    multiply(1, 1)
    w3_on = forward_weight(3, w3)

    across[3].wait_recv()
    across[4].wait_recv()
    multiply(4, 2)
    multiply(0, 2)
    multiply(1, 2)
    for copy in w2_on:
        copy.wait_recv()
    for step in (0, 3, 1, 2):
        multiply(2, step)

    wait_parts(4)
    grad_ranks = rank_own[...]
    for step in (1, 2, 3):
        grad_ranks += rank_in[turn(zl, step)]
    grad_ranks *= 1.0 / math.sqrt(D * 5461.25)
    live_count = counts_ref[0]
    positions = lax.broadcasted_iota(jnp.int32, (RANK, TOK), 1)
    masked = hidden_ranks * jnp.where(positions < live_count, 1.0, 0.0)
    features = lax.dot_general(
        masked, grad_ranks, NT, precision=lax.Precision.HIGHEST, preferred_element_type=jnp.float32
    )
    feat_y[...] = jnp.zeros_like(feat_y)
    for owner in range(32):
        slot = owner // 2 % 4 * 8 + owner // 8 * 2 + owner % 2
        feat_y[slot, 0:2, 0:RANK] = features[owner * 2 : owner * 2 + 2, :]
    y_copies = [
        send(
            feat_y.at[pl.ds(turn(y, step) * 8, 8)], feat_y_in.at[step - 1],
            device(y=turn(y, step)),
        )
        for step in (1, 2, 3)
    ]

    for copy in w3_on:
        copy.wait_recv()
    for step in (0, 3, 1, 2):
        multiply(3, step)

    for copy in y_copies:
        copy.wait_recv()
    feat_z[...] = feat_y[pl.ds(y * 8, 8)] + feat_y_in[0] + feat_y_in[1] + feat_y_in[2]
    z_copies = [
        send(
            feat_z.at[pl.ds(turn(zh, step) * 2, 2)], feat_z_in.at[step - 1],
            device(zh=turn(zh, step)),
        )
        for step in (1, 2, 3)
    ]

    finish(0)
    finish(1)
    for copy in z_copies:
        copy.wait_recv()
    feat_c[...] = feat_z[pl.ds(zh * 2, 2)] + feat_z_in[0] + feat_z_in[1] + feat_z_in[2]
    c_copy = send(feat_c.at[1 - c], feat_c_in, sibling)
    finish(2)
    c_copy.wait_recv()
    counted = jnp.full((8, 128), live_count, jnp.int32).astype(jnp.float32)
    result = (feat_c[c] + feat_c_in[...]) * lax.rsqrt(counted)
    feat_out[0] = result[0:2, 0:RANK]
    finish(3)

    for chunk in range(5):
        for step in range(4):

            @pl.when(turn(y, step) != zl)
            def _(chunk=chunk, step=step):
                part_copy(chunk, step).wait_send()

    for copy in started:
        copy.wait_send()
    for target, remote in crossed:

        @pl.when(target != x)
        def _(remote=remote):
            remote.wait_send()


def shards(grad_out, gate_act, up_act, down_weight, counts, down_seed, up_seed):
    hbm = pl.BlockSpec(memory_space=pltpu.HBM)
    smem = pl.BlockSpec(memory_space=pltpu.SMEM)
    vmem = pl.BlockSpec(memory_space=pltpu.VMEM)
    bf16, f32 = jnp.bfloat16, jnp.float32
    return pl.pallas_call(
        kernel,
        out_shape=(
            jax.ShapeDtypeStruct((TOK, HID), bf16),
            jax.ShapeDtypeStruct((TOK, HID), bf16),
            jax.ShapeDtypeStruct((1, 2, RANK), f32),
        ),
        in_specs=[hbm, hbm, hbm, hbm, smem, smem, smem],
        out_specs=(vmem, vmem, vmem),
        scratch_shapes=[
            pltpu.VMEM((TOK, HID), bf16),
            pltpu.VMEM((TOK, HID), bf16),
            pltpu.VMEM((4, HID, WIDTH), bf16),
            pltpu.VMEM((4, PIECE, WIDTH), bf16),
            pltpu.VMEM((4, 4 * TOK, WIDTH), bf16),
            pltpu.VMEM((4, RANK, WIDTH), bf16),
            pltpu.VMEM((RANK, HID), bf16),
            pltpu.VMEM((TOK, HID), bf16),
            pltpu.VMEM((TOK, HID), f32),
            pltpu.VMEM((TOK, HID), f32),
            pltpu.VMEM((TOK, HID), f32),
            pltpu.VMEM((4, 7, TOK, 128), bf16),
            pltpu.VMEM((4, 7, TOK, 128), bf16),
            pltpu.VMEM((RANK, TOK), f32),
            pltpu.VMEM((4, RANK, TOK), f32),
            pltpu.VMEM((4, RANK, TOK), f32),
            pltpu.VMEM((32, 8, 128), f32),
            pltpu.VMEM((3, 8, 8, 128), f32),
            pltpu.VMEM((8, 8, 128), f32),
            pltpu.VMEM((3, 2, 8, 128), f32),
            pltpu.VMEM((2, 8, 128), f32),
            pltpu.VMEM((8, 128), f32),
            pltpu.SemaphoreType.DMA((COPIES,)),
            pltpu.SemaphoreType.DMA((COPIES,)),
            pltpu.SemaphoreType.DMA((4,)),
            pltpu.SemaphoreType.DMA((4,)),
            pltpu.SemaphoreType.DMA((4,)),
            pltpu.SemaphoreType.DMA((20,)),
            pltpu.SemaphoreType.DMA((20,)),
        ],
        compiler_params=pltpu.CompilerParams(
            collective_id=0, has_side_effects=True, vmem_limit_bytes=60 * 1024 * 1024
        ),
    )(grad_out, gate_act, up_act, down_weight, counts, down_seed, up_seed)


def solution(mesh):
    in_specs = (
        P("col", "row"),
        P("row", "col"),
        P("row", "col"),
        P("col", "row"),
        P("row"),
        P(),
        P(),
    )
    out_specs = (P("row", "col"), P("row", "col"), P("row", "col", None))
    return jax.shard_map(shards, mesh=mesh, in_specs=in_specs, out_specs=out_specs, check_vma=False)
```

```python
import math

import jax
import jax.numpy as jnp
from jax import lax
from jax.experimental import pallas as pl
from jax.experimental.pallas import tpu as pltpu
from jax.sharding import PartitionSpec as P

D = 8192
FF = 28672
RANK = 64
TOK = 128
PIECE = 64
WIDTH = 512
HID = 896
CHUNKS = ((0, 2), (2, 2), (4, 1), (5, 1), (6, 1))
RANKS = len(CHUNKS)
NT = (((1,), (1,)), ((), ()))
MESH = pl.DeviceIdType.MESH
COPIES = 96


def scramble(values):
    values = values ^ values >> 16 & 65535
    values = values * 73244475
    values = values ^ values >> 16 & 65535
    values = values * 73244475
    return values ^ values >> 16 & 65535


def projection_t(seed_value, first_row, row_count):
    row_number = first_row + lax.broadcasted_iota(jnp.int32, (RANK, row_count), 1)
    rank_number = lax.broadcasted_iota(jnp.int32, (RANK, row_count), 0)
    seed_mix = scramble(seed_value + 40503)
    hashed = scramble(row_number * RANK + rank_number ^ seed_mix)
    return ((hashed >> 8 & 255).astype(jnp.float32) - 127.5).astype(jnp.bfloat16)


def kernel(
    grad_ref, gate_ref, up_ref, weight_ref, counts_ref, down_seed_ref, up_seed_ref,
    gate_out, up_out, feat_out,
    gate_in, up_in, weight_in, weights, zblocks, grads, up_proj, down_proj, hidden,
    gate_factor, up_factor, own, part_out, part_in, rank_own, rank_out, rank_in,
    feat_y, feat_y_in, feat_z, feat_z_in, feat_c, feat_c_in,
    send_sem, recv_sem, local_sem, cross_send, cross_recv, part_send, part_recv,
):
    row = lax.axis_index("row")
    col = lax.axis_index("col")
    x, zl = lax.div(row, 4), lax.rem(row, 4)
    zh, y, c = lax.div(col, 8), lax.rem(lax.div(col, 2), 4), lax.rem(col, 2)

    def turn(value, step):
        return lax.rem(value + step, 4)

    def device(x=x, zl=zl, zh=zh, y=y, c=c):
        return (x * 4 + zl, (zh * 4 + y) * 2 + c)

    sibling = device(c=1 - c)
    started = []

    def send(src, dst, target):
        index = len(started)
        copy = pltpu.make_async_remote_copy(
            src_ref=src, dst_ref=dst, send_sem=send_sem.at[index], recv_sem=recv_sem.at[index],
            device_id=target, device_id_type=MESH,
        )
        copy.start()
        started.append(copy)
        return copy

    locals_ = []
    for number, (src, dst) in enumerate(
        ((weight_ref, weight_in), (gate_ref, gate_in), (up_ref, up_in))
    ):
        copy = pltpu.make_async_copy(src, dst, local_sem.at[number])
        copy.start()
        locals_.append(copy)

    barrier = pltpu.get_barrier_semaphore()
    peers = [sibling]
    for step in (1, 2, 3):
        peers += [
            device(x=turn(x, step)), device(zl=turn(zl, step)),
            device(zh=turn(zh, step)), device(y=turn(y, step)),
        ]
    for peer in peers:
        pl.semaphore_signal(barrier, inc=1, device_id=peer, device_id_type=MESH)

    locals_[0].wait()
    for piece in range(2):
        weights[x, piece] = weight_in[piece * 128 : piece * 128 + 128, :].T
    pl.semaphore_wait(barrier, len(peers))


    def mine(group):
        return pl.ds(pl.multiple_of(group * TOK + c * PIECE, PIECE), PIECE)

    def cross(step, src):
        target = turn(zh, step)
        slot = grads.at[x, mine(y)]
        remote = pltpu.make_async_remote_copy(
            src_ref=src, dst_ref=slot, send_sem=cross_send.at[step], recv_sem=cross_recv.at[x],
            device_id=device(x=target), device_id_type=MESH,
        )
        local = pltpu.make_async_copy(src, slot, local_sem.at[3])

        @pl.when(target != x)
        def _():
            remote.start()

        @pl.when(target == x)
        def _():
            local.start()

        return target, remote

    def send_weight(piece):
        block = weights.at[x, piece]
        right = send(block, block, device(x=turn(x, 1)))
        left = send(block, block, device(x=turn(x, 3)))
        return right, left

    def forward_weight(piece, copies):
        right, left = copies
        right.wait_recv()
        block = weights.at[turn(x, 3), piece, pl.ds(0, WIDTH // 2)]
        on_right = send(block, block, device(x=turn(x, 1)))
        left.wait_recv()
        block = weights.at[turn(x, 1), piece, pl.ds(WIDTH // 2, WIDTH // 2)]
        on_left = send(block, block, device(x=turn(x, 3)))
        return on_right, on_left

    def wait_weights(*pieces):
        for copies in pieces:
            for copy in copies:
                copy.wait_recv()

    z_up = send(grad_ref, zblocks.at[zh], device(zh=turn(zh, 1)))
    z_down = send(grad_ref, zblocks.at[zh], device(zh=turn(zh, 3)))
    crossed = [cross(0, grad_ref)]
    w0 = send_weight(0)
    w1 = send_weight(1)

    for piece in range(2, 7):
        weights[x, piece] = weight_in[piece * 128 : piece * 128 + 128, :].T

    down_proj[...] = projection_t(down_seed_ref[0], col * HID, HID)
    for part in range(4):
        up_proj[part] = projection_t(up_seed_ref[0], (part * 4 + zl) * WIDTH, WIDTH)
    locals_[1].wait()
    locals_[2].wait()
    for part in range(7):
        cols = slice(part * 128, part * 128 + 128)
        gate_value = gate_in[:, cols].astype(jnp.float32)
        up_value = up_in[:, cols].astype(jnp.float32)
        sigmoid_gate = jax.nn.sigmoid(gate_value)
        silu_gate = gate_value * sigmoid_gate
        gate_factor[:, cols] = up_value * sigmoid_gate * (1.0 + gate_value * (1.0 - sigmoid_gate))
        up_factor[:, cols] = silu_gate
        hidden[:, cols] = (silu_gate * up_value).astype(jnp.bfloat16)

    w0_on = forward_weight(0, w0)
    z_up.wait_recv()
    block = zblocks.at[turn(zh, 3), pl.ds(0, 32)]
    z_on_up = send(block, block, device(zh=turn(zh, 1)))
    crossed.append(cross(3, zblocks.at[turn(zh, 3)]))
    z_down.wait_recv()
    block = zblocks.at[turn(zh, 1), pl.ds(32, 32)]
    z_on_down = send(block, block, device(zh=turn(zh, 3)))
    crossed.append(cross(1, zblocks.at[turn(zh, 1)]))

    w1_on = forward_weight(1, w1)
    w2 = send_weight(2)
    hidden_ranks = lax.dot_general(
        down_proj[...], hidden[...], NT, preferred_element_type=jnp.float32
    ) * (1.0 / math.sqrt(FF * 5461.25))

    z_on_up.wait_recv()
    z_on_down.wait_recv()
    crossed.append(cross(2, zblocks.at[turn(zh, 2)]))
    w3 = send_weight(3)
    w2_on = forward_weight(2, w2)

    pltpu.make_async_copy(grad_ref, grads.at[x, mine(y)], local_sem.at[3]).wait()
    for step in (1, 2, 3):
        source = turn(x, step)
        slot = grads.at[source, mine(y)]
        pltpu.make_async_remote_copy(
            src_ref=slot, dst_ref=slot, send_sem=cross_send.at[step], recv_sem=cross_recv.at[source],
            device_id=device(x=source), device_id_type=MESH,
        ).wait_recv()

    def y_block(source, first=0, count=4):
        return grads.at[pl.ds(first, count), mine(source)]

    def part_copy(chunk, step):
        target = turn(y, step)
        if chunk == RANKS:
            src, dst = rank_out.at[step], rank_in.at[zl]
        else:
            first, count = CHUNKS[chunk]
            src, dst = part_out.at[step, pl.ds(first, count)], part_in.at[zl, pl.ds(first, count)]
        return pltpu.make_async_remote_copy(
            src_ref=src, dst_ref=dst, send_sem=part_send.at[chunk * 4 + step],
            recv_sem=part_recv.at[chunk * 4 + zl], device_id=device(zl=target), device_id_type=MESH,
        )

    def wait_parts(chunk):
        for step in (1, 2, 3):
            source = turn(zl, step)
            if chunk == RANKS:
                block = rank_in.at[source]
            else:
                first, count = CHUNKS[chunk]
                block = part_in.at[source, pl.ds(first, count)]
            pltpu.make_async_remote_copy(
                src_ref=block, dst_ref=block, send_sem=part_send.at[chunk * 4 + step],
                recv_sem=part_recv.at[chunk * 4 + source], device_id=device(zl=source),
                device_id_type=MESH,
            ).wait_recv()

    def multiply(chunk, step):
        target = turn(y, step)
        tokens = pl.ds(pl.multiple_of(target * TOK, TOK), TOK)
        total = None
        for part in range(4):
            left = grads[part, tokens]
            if chunk == RANKS:
                product = lax.dot_general(
                    left, up_proj[part], NT, preferred_element_type=jnp.float32
                )
            else:
                first, count = CHUNKS[chunk]
                rows = pl.ds(first * 128, count * 128)
                right = [weights[part, first + piece] for piece in range(count)]
                right = jnp.concatenate(right, axis=1) if count > 1 else right[0]
                product = jnp.dot(left, right, preferred_element_type=jnp.float32)
            total = product if part == 0 else total + product

        @pl.when(target == zl)
        def _():
            if chunk == RANKS:
                rank_own[...] = total
            else:
                own[:, rows] = total

        @pl.when(target != zl)
        def _():
            if chunk == RANKS:
                rank_out[step] = total.astype(jnp.bfloat16)
            else:
                for lane in range(count):
                    part_out[step, first + lane] = total[:, lane * 128 : lane * 128 + 128].astype(
                        jnp.bfloat16
                    )
            part_copy(chunk, step).start()

    def finish(chunk):
        wait_parts(chunk)
        first, count = CHUNKS[chunk]
        for lane in range(first, first + count):
            cols = slice(lane * 128, lane * 128 + 128)
            total = own[:, cols]
            for step in (1, 2, 3):
                total += part_in[turn(zl, step), lane].astype(jnp.float32)
            gate_out[:, cols] = (total * gate_factor[:, cols]).astype(jnp.bfloat16)
            up_out[:, cols] = (total * up_factor[:, cols]).astype(jnp.bfloat16)

    block = y_block(y)
    y_up = send(block, block, device(y=turn(y, 1)))
    y_down = send(block, block, device(y=turn(y, 3)))
    across = [send(block, block, sibling)]
    w4 = send_weight(4)
    w3_on = forward_weight(3, w3)

    across[0].wait_recv()
    multiply(RANKS, 0)
    wait_weights(w0_on, w1_on)
    multiply(0, 0)
    w5 = send_weight(5)

    y_up.wait_recv()
    block = y_block(turn(y, 3), 0, 2)
    y_on_up = send(block, block, device(y=turn(y, 1)))
    block = y_block(turn(y, 3))
    across.append(send(block, block, sibling))
    y_down.wait_recv()
    block = y_block(turn(y, 1), 2, 2)
    y_on_down = send(block, block, device(y=turn(y, 3)))
    block = y_block(turn(y, 1))
    across.append(send(block, block, sibling))
    wait_weights(w2_on, w3_on)
    multiply(1, 0)
    w4_on = forward_weight(4, w4)
    w6 = send_weight(6)

    for place, step in ((1, 3), (2, 1)):
        across[place].wait_recv()
        multiply(RANKS, step)
        multiply(0, step)
    y_on_up.wait_recv()
    block = y_block(turn(y, 2), 0, 2)
    across.append(send(block, block, sibling))
    y_on_down.wait_recv()
    block = y_block(turn(y, 2), 2, 2)
    across.append(send(block, block, sibling))
    multiply(1, 3)
    multiply(1, 1)
    w5_on = forward_weight(5, w5)

    across[3].wait_recv()
    across[4].wait_recv()
    multiply(RANKS, 2)
    multiply(0, 2)
    multiply(1, 2)
    wait_weights(w4_on)
    for step in (0, 3, 1, 2):
        multiply(2, step)
    w6_on = forward_weight(6, w6)

    wait_parts(RANKS)
    grad_ranks = rank_own[...]
    for step in (1, 2, 3):
        grad_ranks += rank_in[turn(zl, step)].astype(jnp.float32)
    grad_ranks *= 1.0 / math.sqrt(D * 5461.25)
    live_count = counts_ref[0]
    positions = lax.broadcasted_iota(jnp.int32, (RANK, TOK), 1)
    masked = hidden_ranks * jnp.where(positions < live_count, 1.0, 0.0)
    features = jnp.dot(
        masked, grad_ranks, precision=lax.Precision.HIGHEST, preferred_element_type=jnp.float32
    )
    feat_y[...] = jnp.zeros_like(feat_y)
    for owner in range(32):
        slot = owner // 2 % 4 * 8 + owner // 8 * 2 + owner % 2
        feat_y[slot, 0:2, 0:RANK] = features[owner * 2 : owner * 2 + 2, :]
    y_copies = [
        send(
            feat_y.at[pl.ds(turn(y, step) * 8, 8)], feat_y_in.at[step - 1],
            device(y=turn(y, step)),
        )
        for step in (1, 2, 3)
    ]

    wait_weights(w5_on)
    for step in (0, 3, 1, 2):
        multiply(3, step)
    for copy in y_copies:
        copy.wait_recv()
    feat_z[...] = feat_y[pl.ds(y * 8, 8)] + feat_y_in[0] + feat_y_in[1] + feat_y_in[2]
    z_copies = [
        send(
            feat_z.at[pl.ds(turn(zh, step) * 2, 2)], feat_z_in.at[step - 1],
            device(zh=turn(zh, step)),
        )
        for step in (1, 2, 3)
    ]
    finish(0)

    wait_weights(w6_on)
    for step in (0, 3, 1, 2):
        multiply(4, step)
    finish(1)
    for copy in z_copies:
        copy.wait_recv()
    feat_c[...] = feat_z[pl.ds(zh * 2, 2)] + feat_z_in[0] + feat_z_in[1] + feat_z_in[2]
    c_copy = send(feat_c.at[1 - c], feat_c_in, sibling)
    finish(2)
    c_copy.wait_recv()
    counted = jnp.full((8, 128), live_count, jnp.int32).astype(jnp.float32)
    result = (feat_c[c] + feat_c_in[...]) * lax.rsqrt(counted)
    feat_out[0] = result[0:2, 0:RANK]
    finish(3)
    finish(4)

    for chunk in range(RANKS + 1):
        for step in range(4):

            @pl.when(turn(y, step) != zl)
            def _(chunk=chunk, step=step):
                part_copy(chunk, step).wait_send()

    for copy in started:
        copy.wait_send()
    for target, remote in crossed:

        @pl.when(target != x)
        def _(remote=remote):
            remote.wait_send()


def shards(grad_out, gate_act, up_act, down_weight, counts, down_seed, up_seed):
    hbm = pl.BlockSpec(memory_space=pltpu.HBM)
    smem = pl.BlockSpec(memory_space=pltpu.SMEM)
    vmem = pl.BlockSpec(memory_space=pltpu.VMEM)
    bf16, f32 = jnp.bfloat16, jnp.float32
    return pl.pallas_call(
        kernel,
        out_shape=(
            jax.ShapeDtypeStruct((TOK, HID), bf16),
            jax.ShapeDtypeStruct((TOK, HID), bf16),
            jax.ShapeDtypeStruct((1, 2, RANK), f32),
        ),
        in_specs=[hbm, hbm, hbm, hbm, smem, smem, smem],
        out_specs=(vmem, vmem, vmem),
        scratch_shapes=[
            pltpu.VMEM((TOK, HID), bf16),
            pltpu.VMEM((TOK, HID), bf16),
            pltpu.VMEM((HID, WIDTH), bf16),
            pltpu.VMEM((4, 7, WIDTH, 128), bf16),
            pltpu.VMEM((4, PIECE, WIDTH), bf16),
            pltpu.VMEM((4, 4 * TOK, WIDTH), bf16),
            pltpu.VMEM((4, RANK, WIDTH), bf16),
            pltpu.VMEM((RANK, HID), bf16),
            pltpu.VMEM((TOK, HID), bf16),
            pltpu.VMEM((TOK, HID), f32),
            pltpu.VMEM((TOK, HID), f32),
            pltpu.VMEM((TOK, HID), f32),
            pltpu.VMEM((4, 7, TOK, 128), bf16),
            pltpu.VMEM((4, 7, TOK, 128), bf16),
            pltpu.VMEM((TOK, RANK), f32),
            pltpu.VMEM((4, TOK, RANK), bf16),
            pltpu.VMEM((4, TOK, RANK), bf16),
            pltpu.VMEM((32, 8, 128), f32),
            pltpu.VMEM((3, 8, 8, 128), f32),
            pltpu.VMEM((8, 8, 128), f32),
            pltpu.VMEM((3, 2, 8, 128), f32),
            pltpu.VMEM((2, 8, 128), f32),
            pltpu.VMEM((8, 128), f32),
            pltpu.SemaphoreType.DMA((COPIES,)),
            pltpu.SemaphoreType.DMA((COPIES,)),
            pltpu.SemaphoreType.DMA((4,)),
            pltpu.SemaphoreType.DMA((4,)),
            pltpu.SemaphoreType.DMA((4,)),
            pltpu.SemaphoreType.DMA((4 * RANKS + 4,)),
            pltpu.SemaphoreType.DMA((4 * RANKS + 4,)),
        ],
        compiler_params=pltpu.CompilerParams(
            collective_id=0, has_side_effects=True, vmem_limit_bytes=60 * 1024 * 1024
        ),
    )(grad_out, gate_act, up_act, down_weight, counts, down_seed, up_seed)


def solution(mesh):
    in_specs = (
        P("col", "row"),
        P("row", "col"),
        P("row", "col"),
        P("col", "row"),
        P("row"),
        P(),
        P(),
    )
    out_specs = (P("row", "col"), P("row", "col"), P("row", "col", None))
    return jax.shard_map(shards, mesh=mesh, in_specs=in_specs, out_specs=out_specs, check_vma=False)
```

```python
import math

import jax
import jax.numpy as jnp
from jax import lax
from jax.experimental import pallas as pl
from jax.experimental.pallas import tpu as pltpu
from jax.sharding import PartitionSpec as P

D = 8192
FF = 28672
RANK = 64
TOK = 128
PIECE = 64
WIDTH = 512
HID = 896
CHUNKS = ((0, 2), (2, 2), (4, 1), (5, 1), (6, 1))
RANKS = len(CHUNKS)
NT = (((1,), (1,)), ((), ()))
MESH = pl.DeviceIdType.MESH
COPIES = 96


def scramble(values):
    values = values ^ values >> 16 & 65535
    values = values * 73244475
    values = values ^ values >> 16 & 65535
    values = values * 73244475
    return values ^ values >> 16 & 65535


def projection_t(seed_value, first_row, row_count):
    row_number = first_row + lax.broadcasted_iota(jnp.int32, (RANK, row_count), 1)
    rank_number = lax.broadcasted_iota(jnp.int32, (RANK, row_count), 0)
    seed_mix = scramble(seed_value + 40503)
    hashed = scramble(row_number * RANK + rank_number ^ seed_mix)
    return ((hashed >> 8 & 255).astype(jnp.float32) - 127.5).astype(jnp.bfloat16)


def kernel(
    grad_ref, gate_ref, up_ref, weight_ref, counts_ref, down_seed_ref, up_seed_ref,
    gate_out, up_out, feat_out,
    gate_in, up_in, weight_in, weights, zblocks, grads, up_proj, down_proj, hidden,
    gate_factor, up_factor, own, part_out, part_on, part_in, rank_own, rank_out, rank_on, rank_in,
    feat_y, feat_y_in, feat_z, feat_z_in, feat_c, feat_c_in,
    send_sem, recv_sem, local_sem, cross_send, cross_recv, part_send, part_recv,
):
    row = lax.axis_index("row")
    col = lax.axis_index("col")
    x, zl = lax.div(row, 4), lax.rem(row, 4)
    zh, y, c = lax.div(col, 8), lax.rem(lax.div(col, 2), 4), lax.rem(col, 2)

    def turn(value, step):
        return lax.rem(value + step, 4)

    def device(x=x, zl=zl, zh=zh, y=y, c=c):
        return (x * 4 + zl, (zh * 4 + y) * 2 + c)

    sibling = device(c=1 - c)
    started = []

    def send(src, dst, target):
        index = len(started)
        copy = pltpu.make_async_remote_copy(
            src_ref=src, dst_ref=dst, send_sem=send_sem.at[index], recv_sem=recv_sem.at[index],
            device_id=target, device_id_type=MESH,
        )
        copy.start()
        started.append(copy)
        return copy

    locals_ = []
    for number, (src, dst) in enumerate(
        ((weight_ref, weight_in), (gate_ref, gate_in), (up_ref, up_in))
    ):
        copy = pltpu.make_async_copy(src, dst, local_sem.at[number])
        copy.start()
        locals_.append(copy)

    barrier = pltpu.get_barrier_semaphore()
    peers = [sibling]
    for step in (1, 2, 3):
        peers += [
            device(x=turn(x, step)), device(zl=turn(zl, step)),
            device(zh=turn(zh, step)), device(y=turn(y, step)),
        ]
    for peer in peers:
        pl.semaphore_signal(barrier, inc=1, device_id=peer, device_id_type=MESH)

    locals_[0].wait()
    for piece in range(2):
        weights[x, piece] = weight_in[piece * 128 : piece * 128 + 128, :].T
    pl.semaphore_wait(barrier, len(peers))


    def mine(group):
        return pl.ds(pl.multiple_of(group * TOK + c * PIECE, PIECE), PIECE)

    def cross(step, src):
        target = turn(zh, step)
        slot = grads.at[x, mine(y)]
        remote = pltpu.make_async_remote_copy(
            src_ref=src, dst_ref=slot, send_sem=cross_send.at[step], recv_sem=cross_recv.at[x],
            device_id=device(x=target), device_id_type=MESH,
        )
        local = pltpu.make_async_copy(src, slot, local_sem.at[3])

        @pl.when(target != x)
        def _():
            remote.start()

        @pl.when(target == x)
        def _():
            local.start()

        return target, remote

    def send_weight(piece):
        block = weights.at[x, piece]
        right = send(block, block, device(x=turn(x, 1)))
        left = send(block, block, device(x=turn(x, 3)))
        return right, left

    def forward_weight(piece, copies):
        right, left = copies
        right.wait_recv()
        block = weights.at[turn(x, 3), piece, pl.ds(0, WIDTH // 2)]
        on_right = send(block, block, device(x=turn(x, 1)))
        left.wait_recv()
        block = weights.at[turn(x, 1), piece, pl.ds(WIDTH // 2, WIDTH // 2)]
        on_left = send(block, block, device(x=turn(x, 3)))
        return on_right, on_left

    def wait_weights(*pieces):
        for copies in pieces:
            for copy in copies:
                copy.wait_recv()

    z_up = send(grad_ref, zblocks.at[zh], device(zh=turn(zh, 1)))
    z_down = send(grad_ref, zblocks.at[zh], device(zh=turn(zh, 3)))
    crossed = [cross(0, grad_ref)]
    w0 = send_weight(0)
    w1 = send_weight(1)

    for piece in range(2, 7):
        weights[x, piece] = weight_in[piece * 128 : piece * 128 + 128, :].T

    down_proj[...] = projection_t(down_seed_ref[0], col * HID, HID)
    for part in range(4):
        up_proj[part] = projection_t(up_seed_ref[0], (part * 4 + zl) * WIDTH, WIDTH)
    locals_[1].wait()
    locals_[2].wait()
    for part in range(7):
        cols = slice(part * 128, part * 128 + 128)
        gate_value = gate_in[:, cols].astype(jnp.float32)
        up_value = up_in[:, cols].astype(jnp.float32)
        sigmoid_gate = jax.nn.sigmoid(gate_value)
        silu_gate = gate_value * sigmoid_gate
        gate_factor[:, cols] = up_value * sigmoid_gate * (1.0 + gate_value * (1.0 - sigmoid_gate))
        up_factor[:, cols] = silu_gate
        hidden[:, cols] = (silu_gate * up_value).astype(jnp.bfloat16)

    w0_on = forward_weight(0, w0)
    z_up.wait_recv()
    block = zblocks.at[turn(zh, 3), pl.ds(0, 32)]
    z_on_up = send(block, block, device(zh=turn(zh, 1)))
    crossed.append(cross(3, zblocks.at[turn(zh, 3)]))
    z_down.wait_recv()
    block = zblocks.at[turn(zh, 1), pl.ds(32, 32)]
    z_on_down = send(block, block, device(zh=turn(zh, 3)))
    crossed.append(cross(1, zblocks.at[turn(zh, 1)]))

    w1_on = forward_weight(1, w1)
    w2 = send_weight(2)
    hidden_ranks = lax.dot_general(
        down_proj[...], hidden[...], NT, preferred_element_type=jnp.float32
    ) * (1.0 / math.sqrt(FF * 5461.25))

    z_on_up.wait_recv()
    z_on_down.wait_recv()
    crossed.append(cross(2, zblocks.at[turn(zh, 2)]))
    w3 = send_weight(3)
    w2_on = forward_weight(2, w2)

    pltpu.make_async_copy(grad_ref, grads.at[x, mine(y)], local_sem.at[3]).wait()
    for step in (1, 2, 3):
        source = turn(x, step)
        slot = grads.at[source, mine(y)]
        pltpu.make_async_remote_copy(
            src_ref=slot, dst_ref=slot, send_sem=cross_send.at[step], recv_sem=cross_recv.at[source],
            device_id=device(x=source), device_id_type=MESH,
        ).wait_recv()

    def y_block(source, first=0, count=4):
        return grads.at[pl.ds(first, count), mine(source)]

    side, inner = lax.div(zl, 2), lax.rem(zl + lax.div(zl, 2), 2) == 1
    mate = side * 2 + 1 - lax.rem(zl, 2)

    def is_across(target):
        return lax.div(target, 2) != side

    def part_copy(chunk, kind, target):
        if chunk == RANKS:
            at = ()
        else:
            at = (pl.ds(*CHUNKS[chunk]),)
        src = (rank_out if chunk == RANKS else part_out).at[(target,) + at]
        if kind == 1:
            slot = lax.rem(target, 2)
            dst = (rank_on if chunk == RANKS else part_on).at[(slot,) + at]
            sem = 2 + slot
        else:
            slot = 0 if kind == 0 else 1
            dst = (rank_in if chunk == RANKS else part_in).at[(slot,) + at]
            sem = slot
        return pltpu.make_async_remote_copy(
            src_ref=src, dst_ref=dst, send_sem=part_send.at[chunk * 4 + target],
            recv_sem=part_recv.at[chunk * 4 + sem],
            device_id=device(zl=target if kind == 2 else mate), device_id_type=MESH,
        )

    def wait_parts(chunk):
        part_copy(chunk, 0, mate).wait_recv()
        part_copy(chunk, 2, lax.rem(zl + 2, 4)).wait_recv()

    def put(chunk, target, total):
        if chunk == RANKS:
            rank_out[target] = total.astype(jnp.bfloat16)
        else:
            first, count = CHUNKS[chunk]
            for lane in range(count):
                part_out[target, first + lane] = total[:, lane * 128 : lane * 128 + 128].astype(
                    jnp.bfloat16
                )

    pending = []

    def multiply(chunk, target):
        tokens = pl.ds(pl.multiple_of(target * TOK, TOK), TOK)
        total = None
        for part in range(4):
            left = grads[part, tokens]
            if chunk == RANKS:
                product = lax.dot_general(
                    left, up_proj[part], NT, preferred_element_type=jnp.float32
                )
            else:
                first, count = CHUNKS[chunk]
                right = [weights[part, first + piece] for piece in range(count)]
                right = jnp.concatenate(right, axis=1) if count > 1 else right[0]
                product = jnp.dot(left, right, preferred_element_type=jnp.float32)
            total = product if part == 0 else total + product

        keep = (target == zl) | (is_across(target) & inner)

        @pl.when(keep)
        def _():
            if chunk == RANKS:
                rank_own[target] = total
            else:
                own[target, :, first * 128 : (first + count) * 128] = total

        @pl.when(target == mate)
        def _():
            put(chunk, target, total)
            part_copy(chunk, 0, target).start()

        @pl.when(is_across(target) & jnp.logical_not(inner))
        def _():
            put(chunk, target, total)
            part_copy(chunk, 1, target).start()

        pending.append((chunk, target))

    def relay(most=0):
        while len(pending) > most:
            chunk, target = pending.pop(0)

            @pl.when(is_across(target) & inner)
            def _(chunk=chunk, target=target):
                part_copy(chunk, 1, target).wait_recv()
                slot = lax.rem(target, 2)
                if chunk == RANKS:
                    put(chunk, target, rank_own[target] + rank_on[slot].astype(jnp.float32))
                else:
                    first, count = CHUNKS[chunk]
                    for lane in range(first, first + count):
                        part_out[target, lane] = (
                            own[target, :, lane * 128 : lane * 128 + 128]
                            + part_on[slot, lane].astype(jnp.float32)
                        ).astype(jnp.bfloat16)
                part_copy(chunk, 2, target).start()

    def multiply_all(chunk):
        for target in (2 - side * 2, 3 - side * 2, mate, zl):
            multiply(chunk, target)

    def finish(chunk):
        wait_parts(chunk)
        first, count = CHUNKS[chunk]
        for lane in range(first, first + count):
            cols = slice(lane * 128, lane * 128 + 128)
            total = own[zl, :, cols]
            for source in range(2):
                total += part_in[source, lane].astype(jnp.float32)
            gate_out[:, cols] = (total * gate_factor[:, cols]).astype(jnp.bfloat16)
            up_out[:, cols] = (total * up_factor[:, cols]).astype(jnp.bfloat16)

    block = y_block(y)
    y_up = send(block, block, device(y=turn(y, 1)))
    y_down = send(block, block, device(y=turn(y, 3)))
    across = [send(block, block, sibling)]
    w4 = send_weight(4)
    w3_on = forward_weight(3, w3)

    across[0].wait_recv()
    multiply(RANKS, turn(y, 0))
    wait_weights(w0_on, w1_on)
    multiply(0, turn(y, 0))
    w5 = send_weight(5)

    relay()
    y_up.wait_recv()
    block = y_block(turn(y, 3), 0, 2)
    y_on_up = send(block, block, device(y=turn(y, 1)))
    block = y_block(turn(y, 3))
    across.append(send(block, block, sibling))
    y_down.wait_recv()
    block = y_block(turn(y, 1), 2, 2)
    y_on_down = send(block, block, device(y=turn(y, 3)))
    block = y_block(turn(y, 1))
    across.append(send(block, block, sibling))
    wait_weights(w2_on, w3_on)
    multiply(1, turn(y, 0))
    relay()
    w4_on = forward_weight(4, w4)
    w6 = send_weight(6)

    for place, step in ((1, 3), (2, 1)):
        across[place].wait_recv()
        multiply(RANKS, turn(y, step))
        multiply(0, turn(y, step))
        relay(2)
    y_on_up.wait_recv()
    block = y_block(turn(y, 2), 0, 2)
    across.append(send(block, block, sibling))
    y_on_down.wait_recv()
    block = y_block(turn(y, 2), 2, 2)
    across.append(send(block, block, sibling))
    multiply(1, turn(y, 3))
    multiply(1, turn(y, 1))
    relay()
    w5_on = forward_weight(5, w5)

    across[3].wait_recv()
    across[4].wait_recv()
    multiply(RANKS, turn(y, 2))
    multiply(0, turn(y, 2))
    relay(2)
    multiply(1, turn(y, 2))
    wait_weights(w4_on)
    multiply_all(2)
    relay()
    w6_on = forward_weight(6, w6)

    wait_parts(RANKS)
    grad_ranks = rank_own[zl]
    for source in range(2):
        grad_ranks += rank_in[source].astype(jnp.float32)
    grad_ranks *= 1.0 / math.sqrt(D * 5461.25)
    live_count = counts_ref[0]
    positions = lax.broadcasted_iota(jnp.int32, (RANK, TOK), 1)
    masked = hidden_ranks * jnp.where(positions < live_count, 1.0, 0.0)
    features = jnp.dot(
        masked, grad_ranks, precision=lax.Precision.HIGHEST, preferred_element_type=jnp.float32
    )
    feat_y[...] = jnp.zeros_like(feat_y)
    for owner in range(32):
        slot = owner // 2 % 4 * 8 + owner // 8 * 2 + owner % 2
        feat_y[slot, 0:2, 0:RANK] = features[owner * 2 : owner * 2 + 2, :]
    y_copies = [
        send(
            feat_y.at[pl.ds(turn(y, step) * 8, 8)], feat_y_in.at[step - 1],
            device(y=turn(y, step)),
        )
        for step in (1, 2, 3)
    ]

    wait_weights(w5_on)
    multiply_all(3)
    relay()
    for copy in y_copies:
        copy.wait_recv()
    feat_z[...] = feat_y[pl.ds(y * 8, 8)] + feat_y_in[0] + feat_y_in[1] + feat_y_in[2]
    z_copies = [
        send(
            feat_z.at[pl.ds(turn(zh, step) * 2, 2)], feat_z_in.at[step - 1],
            device(zh=turn(zh, step)),
        )
        for step in (1, 2, 3)
    ]
    finish(0)

    wait_weights(w6_on)
    multiply_all(4)
    relay()
    finish(1)
    for copy in z_copies:
        copy.wait_recv()
    feat_c[...] = feat_z[pl.ds(zh * 2, 2)] + feat_z_in[0] + feat_z_in[1] + feat_z_in[2]
    c_copy = send(feat_c.at[1 - c], feat_c_in, sibling)
    finish(2)
    c_copy.wait_recv()
    counted = jnp.full((8, 128), live_count, jnp.int32).astype(jnp.float32)
    result = (feat_c[c] + feat_c_in[...]) * lax.rsqrt(counted)
    feat_out[0] = result[0:2, 0:RANK]
    finish(3)
    finish(4)

    for chunk in range(RANKS + 1):
        for target in range(4):

            @pl.when(zl != target)
            def _(chunk=chunk, target=target):
                part_copy(chunk, 2, target).wait_send()

    for copy in started:
        copy.wait_send()
    for target, remote in crossed:

        @pl.when(target != x)
        def _(remote=remote):
            remote.wait_send()


def shards(grad_out, gate_act, up_act, down_weight, counts, down_seed, up_seed):
    hbm = pl.BlockSpec(memory_space=pltpu.HBM)
    smem = pl.BlockSpec(memory_space=pltpu.SMEM)
    vmem = pl.BlockSpec(memory_space=pltpu.VMEM)
    bf16, f32 = jnp.bfloat16, jnp.float32
    return pl.pallas_call(
        kernel,
        out_shape=(
            jax.ShapeDtypeStruct((TOK, HID), bf16),
            jax.ShapeDtypeStruct((TOK, HID), bf16),
            jax.ShapeDtypeStruct((1, 2, RANK), f32),
        ),
        in_specs=[hbm, hbm, hbm, hbm, smem, smem, smem],
        out_specs=(vmem, vmem, vmem),
        scratch_shapes=[
            pltpu.VMEM((TOK, HID), bf16),
            pltpu.VMEM((TOK, HID), bf16),
            pltpu.VMEM((HID, WIDTH), bf16),
            pltpu.VMEM((4, 7, WIDTH, 128), bf16),
            pltpu.VMEM((4, PIECE, WIDTH), bf16),
            pltpu.VMEM((4, 4 * TOK, WIDTH), bf16),
            pltpu.VMEM((4, RANK, WIDTH), bf16),
            pltpu.VMEM((RANK, HID), bf16),
            pltpu.VMEM((TOK, HID), bf16),
            pltpu.VMEM((TOK, HID), f32),
            pltpu.VMEM((TOK, HID), f32),
            pltpu.VMEM((4, TOK, HID), f32),
            pltpu.VMEM((4, 7, TOK, 128), bf16),
            pltpu.VMEM((2, 7, TOK, 128), bf16),
            pltpu.VMEM((2, 7, TOK, 128), bf16),
            pltpu.VMEM((4, TOK, RANK), f32),
            pltpu.VMEM((4, TOK, RANK), bf16),
            pltpu.VMEM((2, TOK, RANK), bf16),
            pltpu.VMEM((2, TOK, RANK), bf16),
            pltpu.VMEM((32, 8, 128), f32),
            pltpu.VMEM((3, 8, 8, 128), f32),
            pltpu.VMEM((8, 8, 128), f32),
            pltpu.VMEM((3, 2, 8, 128), f32),
            pltpu.VMEM((2, 8, 128), f32),
            pltpu.VMEM((8, 128), f32),
            pltpu.SemaphoreType.DMA((COPIES,)),
            pltpu.SemaphoreType.DMA((COPIES,)),
            pltpu.SemaphoreType.DMA((4,)),
            pltpu.SemaphoreType.DMA((4,)),
            pltpu.SemaphoreType.DMA((4,)),
            pltpu.SemaphoreType.DMA((4 * RANKS + 4,)),
            pltpu.SemaphoreType.DMA((4 * RANKS + 4,)),
        ],
        compiler_params=pltpu.CompilerParams(
            collective_id=0, has_side_effects=True, vmem_limit_bytes=60 * 1024 * 1024
        ),
    )(grad_out, gate_act, up_act, down_weight, counts, down_seed, up_seed)


def solution(mesh):
    in_specs = (
        P("col", "row"),
        P("row", "col"),
        P("row", "col"),
        P("col", "row"),
        P("row"),
        P(),
        P(),
    )
    out_specs = (P("row", "col"), P("row", "col"), P("row", "col", None))
    return jax.shard_map(shards, mesh=mesh, in_specs=in_specs, out_specs=out_specs, check_vma=False)
```

```python
import math

import jax
import jax.numpy as jnp
from jax import lax
from jax.experimental import pallas as pl
from jax.experimental.pallas import tpu as pltpu
from jax.sharding import PartitionSpec as P

D = 8192
FF = 28672
RANK = 64
TOK = 128
PIECE = 64
WIDTH = 512
HID = 896
CHUNKS = ((0, 2), (2, 2), (4, 1), (5, 1), (6, 1))
RANKS = len(CHUNKS)
NT = (((1,), (1,)), ((), ()))
MESH = pl.DeviceIdType.MESH
COPIES = 96


def scramble(values):
    values = values ^ values >> 16 & 65535
    values = values * 73244475
    values = values ^ values >> 16 & 65535
    values = values * 73244475
    return values ^ values >> 16 & 65535


def projection_t(seed_value, first_row, row_count):
    row_number = first_row + lax.broadcasted_iota(jnp.int32, (RANK, row_count), 1)
    rank_number = lax.broadcasted_iota(jnp.int32, (RANK, row_count), 0)
    seed_mix = scramble(seed_value + 40503)
    hashed = scramble(row_number * RANK + rank_number ^ seed_mix)
    return ((hashed >> 8 & 255).astype(jnp.float32) - 127.5).astype(jnp.bfloat16)


def kernel(
    grad_ref, gate_ref, up_ref, weight_ref, counts_ref, down_seed_ref, up_seed_ref,
    gate_out, up_out, feat_out,
    gate_in, up_in, weight_in, weights, zblocks, grads, up_proj, down_proj, hidden,
    gate_factor, up_factor, own, part_out, part_in, rank_own, rank_out, rank_in,
    feat_y, feat_y_in, feat_z, feat_z_in, feat_c, feat_c_in,
    send_sem, recv_sem, local_sem, cross_send, cross_recv, part_send, part_recv,
):
    row = lax.axis_index("row")
    col = lax.axis_index("col")
    x, zl = lax.div(row, 4), lax.rem(row, 4)
    zh, y, c = lax.div(col, 8), lax.rem(lax.div(col, 2), 4), lax.rem(col, 2)

    def turn(value, step):
        return lax.rem(value + step, 4)

    def device(x=x, zl=zl, zh=zh, y=y, c=c):
        return (x * 4 + zl, (zh * 4 + y) * 2 + c)

    sibling = device(c=1 - c)
    started = []

    def send(src, dst, target):
        index = len(started)
        copy = pltpu.make_async_remote_copy(
            src_ref=src, dst_ref=dst, send_sem=send_sem.at[index], recv_sem=recv_sem.at[index],
            device_id=target, device_id_type=MESH,
        )
        copy.start()
        started.append(copy)
        return copy

    locals_ = []
    for number, (src, dst) in enumerate(
        ((weight_ref, weight_in), (gate_ref, gate_in), (up_ref, up_in))
    ):
        copy = pltpu.make_async_copy(src, dst, local_sem.at[number])
        copy.start()
        locals_.append(copy)

    barrier = pltpu.get_barrier_semaphore()
    peers = [sibling]
    for step in (1, 2, 3):
        peers += [
            device(x=turn(x, step)), device(zl=turn(zl, step)),
            device(zh=turn(zh, step)), device(y=turn(y, step)),
        ]
    for peer in peers:
        pl.semaphore_signal(barrier, inc=1, device_id=peer, device_id_type=MESH)

    locals_[0].wait()
    def turn_weight(*pieces):
        for piece in pieces:
            weights[x, piece] = weight_in[piece * 128 : piece * 128 + 128, :].T

    turn_weight(0, 1)
    pl.semaphore_wait(barrier, len(peers))


    def mine(group):
        return pl.ds(pl.multiple_of(group * TOK + c * PIECE, PIECE), PIECE)

    def cross(step, src):
        target = turn(zh, step)
        slot = grads.at[x, mine(y)]
        remote = pltpu.make_async_remote_copy(
            src_ref=src, dst_ref=slot, send_sem=cross_send.at[step], recv_sem=cross_recv.at[x],
            device_id=device(x=target), device_id_type=MESH,
        )
        local = pltpu.make_async_copy(src, slot, local_sem.at[3])

        @pl.when(target != x)
        def _():
            remote.start()

        @pl.when(target == x)
        def _():
            local.start()

        return target, remote

    def send_weight(piece):
        block = weights.at[x, piece]
        right = send(block, block, device(x=turn(x, 1)))
        left = send(block, block, device(x=turn(x, 3)))
        return right, left

    def forward_weight(piece, copies):
        right, left = copies
        right.wait_recv()
        block = weights.at[turn(x, 3), piece, pl.ds(0, WIDTH // 2)]
        on_right = send(block, block, device(x=turn(x, 1)))
        left.wait_recv()
        block = weights.at[turn(x, 1), piece, pl.ds(WIDTH // 2, WIDTH // 2)]
        on_left = send(block, block, device(x=turn(x, 3)))
        return on_right, on_left

    def wait_weights(*pieces):
        for copies in pieces:
            for copy in copies:
                copy.wait_recv()

    z_up = send(grad_ref, zblocks.at[zh], device(zh=turn(zh, 1)))
    z_down = send(grad_ref, zblocks.at[zh], device(zh=turn(zh, 3)))
    crossed = [cross(0, grad_ref)]
    w0 = send_weight(0)
    w1 = send_weight(1)

    turn_weight(2)
    locals_[1].wait()
    locals_[2].wait()
    for part in range(7):
        cols = slice(part * 128, part * 128 + 128)
        gate_value = gate_in[:, cols].astype(jnp.float32)
        up_value = up_in[:, cols].astype(jnp.float32)
        sigmoid_gate = jax.nn.sigmoid(gate_value)
        silu_gate = gate_value * sigmoid_gate
        gate_factor[:, cols] = up_value * sigmoid_gate * (1.0 + gate_value * (1.0 - sigmoid_gate))
        up_factor[:, cols] = silu_gate
        hidden[:, cols] = (silu_gate * up_value).astype(jnp.bfloat16)

    z_up.wait_recv()
    block = zblocks.at[turn(zh, 3), pl.ds(0, 32)]
    z_on_up = send(block, block, device(zh=turn(zh, 1)))
    crossed.append(cross(3, zblocks.at[turn(zh, 3)]))
    z_down.wait_recv()
    block = zblocks.at[turn(zh, 1), pl.ds(32, 32)]
    z_on_down = send(block, block, device(zh=turn(zh, 3)))
    crossed.append(cross(1, zblocks.at[turn(zh, 1)]))

    w0_on = forward_weight(0, w0)
    w1_on = forward_weight(1, w1)
    w2 = send_weight(2)
    turn_weight(3, 4)
    for part in range(4):
        up_proj[part] = projection_t(up_seed_ref[0], (part * 4 + zl) * WIDTH, WIDTH)

    z_on_up.wait_recv()
    z_on_down.wait_recv()
    crossed.append(cross(2, zblocks.at[turn(zh, 2)]))
    w3 = send_weight(3)
    w2_on = forward_weight(2, w2)
    turn_weight(5, 6)
    down_proj[...] = projection_t(down_seed_ref[0], col * HID, HID)
    hidden_ranks = lax.dot_general(
        down_proj[...], hidden[...], NT, preferred_element_type=jnp.float32
    ) * (1.0 / math.sqrt(FF * 5461.25))

    pltpu.make_async_copy(grad_ref, grads.at[x, mine(y)], local_sem.at[3]).wait()
    for step in (1, 2, 3):
        source = turn(x, step)
        slot = grads.at[source, mine(y)]
        pltpu.make_async_remote_copy(
            src_ref=slot, dst_ref=slot, send_sem=cross_send.at[step], recv_sem=cross_recv.at[source],
            device_id=device(x=source), device_id_type=MESH,
        ).wait_recv()

    def y_block(source, first=0, count=4):
        return grads.at[pl.ds(first, count), mine(source)]

    def part_copy(chunk, step):
        target = turn(y, step)
        if chunk == RANKS:
            src, dst = rank_out.at[step], rank_in.at[zl]
        else:
            first, count = CHUNKS[chunk]
            src, dst = part_out.at[step, pl.ds(first, count)], part_in.at[zl, pl.ds(first, count)]
        return pltpu.make_async_remote_copy(
            src_ref=src, dst_ref=dst, send_sem=part_send.at[chunk * 4 + step],
            recv_sem=part_recv.at[chunk * 4 + zl], device_id=device(zl=target), device_id_type=MESH,
        )

    def wait_parts(chunk):
        for step in (1, 2, 3):
            source = turn(zl, step)
            if chunk == RANKS:
                block = rank_in.at[source]
            else:
                first, count = CHUNKS[chunk]
                block = part_in.at[source, pl.ds(first, count)]
            pltpu.make_async_remote_copy(
                src_ref=block, dst_ref=block, send_sem=part_send.at[chunk * 4 + step],
                recv_sem=part_recv.at[chunk * 4 + source], device_id=device(zl=source),
                device_id_type=MESH,
            ).wait_recv()

    def multiply(chunk, step):
        target = turn(y, step)
        tokens = pl.ds(pl.multiple_of(target * TOK, TOK), TOK)
        total = None
        for part in range(4):
            left = grads[part, tokens]
            if chunk == RANKS:
                product = lax.dot_general(
                    left, up_proj[part], NT, preferred_element_type=jnp.float32
                )
            else:
                first, count = CHUNKS[chunk]
                rows = pl.ds(first * 128, count * 128)
                right = [weights[part, first + piece] for piece in range(count)]
                right = jnp.concatenate(right, axis=1) if count > 1 else right[0]
                product = jnp.dot(left, right, preferred_element_type=jnp.float32)
            total = product if part == 0 else total + product

        @pl.when(target == zl)
        def _():
            if chunk == RANKS:
                rank_own[...] = total
            else:
                own[:, rows] = total

        @pl.when(target != zl)
        def _():
            if chunk == RANKS:
                rank_out[step] = total.astype(jnp.bfloat16)
            else:
                for lane in range(count):
                    part_out[step, first + lane] = total[:, lane * 128 : lane * 128 + 128].astype(
                        jnp.bfloat16
                    )
            part_copy(chunk, step).start()

    def finish(chunk):
        wait_parts(chunk)
        first, count = CHUNKS[chunk]
        for lane in range(first, first + count):
            cols = slice(lane * 128, lane * 128 + 128)
            total = own[:, cols]
            for step in (1, 2, 3):
                total += part_in[turn(zl, step), lane].astype(jnp.float32)
            gate_out[:, cols] = (total * gate_factor[:, cols]).astype(jnp.bfloat16)
            up_out[:, cols] = (total * up_factor[:, cols]).astype(jnp.bfloat16)

    block = y_block(y)
    y_up = send(block, block, device(y=turn(y, 1)))
    y_down = send(block, block, device(y=turn(y, 3)))
    across = [send(block, block, sibling)]
    w4 = send_weight(4)
    w3_on = forward_weight(3, w3)

    across[0].wait_recv()
    multiply(RANKS, 0)
    wait_weights(w0_on, w1_on)
    multiply(0, 0)
    w5 = send_weight(5)

    y_up.wait_recv()
    block = y_block(turn(y, 3), 0, 2)
    y_on_up = send(block, block, device(y=turn(y, 1)))
    block = y_block(turn(y, 3))
    across.append(send(block, block, sibling))
    y_down.wait_recv()
    block = y_block(turn(y, 1), 2, 2)
    y_on_down = send(block, block, device(y=turn(y, 3)))
    block = y_block(turn(y, 1))
    across.append(send(block, block, sibling))
    wait_weights(w2_on, w3_on)
    multiply(1, 0)
    w4_on = forward_weight(4, w4)
    w6 = send_weight(6)

    for place, step in ((1, 3), (2, 1)):
        across[place].wait_recv()
        multiply(RANKS, step)
        multiply(0, step)
    y_on_up.wait_recv()
    block = y_block(turn(y, 2), 0, 2)
    across.append(send(block, block, sibling))
    y_on_down.wait_recv()
    block = y_block(turn(y, 2), 2, 2)
    across.append(send(block, block, sibling))
    multiply(1, 3)
    multiply(1, 1)
    w5_on = forward_weight(5, w5)

    across[3].wait_recv()
    across[4].wait_recv()
    multiply(RANKS, 2)
    multiply(0, 2)
    multiply(1, 2)
    wait_weights(w4_on)
    for step in (0, 3, 1, 2):
        multiply(2, step)
    w6_on = forward_weight(6, w6)

    wait_parts(RANKS)
    grad_ranks = rank_own[...]
    for step in (1, 2, 3):
        grad_ranks += rank_in[turn(zl, step)].astype(jnp.float32)
    grad_ranks *= 1.0 / math.sqrt(D * 5461.25)
    live_count = counts_ref[0]
    positions = lax.broadcasted_iota(jnp.int32, (RANK, TOK), 1)
    masked = hidden_ranks * jnp.where(positions < live_count, 1.0, 0.0)
    features = jnp.dot(
        masked, grad_ranks, precision=lax.Precision.HIGHEST, preferred_element_type=jnp.float32
    )
    feat_y[...] = jnp.zeros_like(feat_y)
    for owner in range(32):
        slot = owner // 2 % 4 * 8 + owner // 8 * 2 + owner % 2
        feat_y[slot, 0:2, 0:RANK] = features[owner * 2 : owner * 2 + 2, :]
    y_copies = [
        send(
            feat_y.at[pl.ds(turn(y, step) * 8, 8)], feat_y_in.at[step - 1],
            device(y=turn(y, step)),
        )
        for step in (1, 2, 3)
    ]

    wait_weights(w5_on)
    for step in (0, 3, 1, 2):
        multiply(3, step)
    for copy in y_copies:
        copy.wait_recv()
    feat_z[...] = feat_y[pl.ds(y * 8, 8)] + feat_y_in[0] + feat_y_in[1] + feat_y_in[2]
    z_copies = [
        send(
            feat_z.at[pl.ds(turn(zh, step) * 2, 2)], feat_z_in.at[step - 1],
            device(zh=turn(zh, step)),
        )
        for step in (1, 2, 3)
    ]
    finish(0)

    wait_weights(w6_on)
    for step in (0, 3, 1, 2):
        multiply(4, step)
    finish(1)
    for copy in z_copies:
        copy.wait_recv()
    feat_c[...] = feat_z[pl.ds(zh * 2, 2)] + feat_z_in[0] + feat_z_in[1] + feat_z_in[2]
    c_copy = send(feat_c.at[1 - c], feat_c_in, sibling)
    finish(2)
    c_copy.wait_recv()
    counted = jnp.full((8, 128), live_count, jnp.int32).astype(jnp.float32)
    result = (feat_c[c] + feat_c_in[...]) * lax.rsqrt(counted)
    feat_out[0] = result[0:2, 0:RANK]
    finish(3)
    finish(4)

    for chunk in range(RANKS + 1):
        for step in range(4):

            @pl.when(turn(y, step) != zl)
            def _(chunk=chunk, step=step):
                part_copy(chunk, step).wait_send()

    for copy in started:
        copy.wait_send()
    for target, remote in crossed:

        @pl.when(target != x)
        def _(remote=remote):
            remote.wait_send()


def shards(grad_out, gate_act, up_act, down_weight, counts, down_seed, up_seed):
    hbm = pl.BlockSpec(memory_space=pltpu.HBM)
    smem = pl.BlockSpec(memory_space=pltpu.SMEM)
    vmem = pl.BlockSpec(memory_space=pltpu.VMEM)
    bf16, f32 = jnp.bfloat16, jnp.float32
    return pl.pallas_call(
        kernel,
        out_shape=(
            pltpu.VMEM((TOK, HID), bf16),
            pltpu.VMEM((TOK, HID), bf16),
            pltpu.VMEM((1, 2, RANK), f32),
        ),
        in_specs=[hbm, hbm, hbm, hbm, smem, smem, smem],
        out_specs=(vmem, vmem, vmem),
        scratch_shapes=[
            pltpu.VMEM((TOK, HID), bf16),
            pltpu.VMEM((TOK, HID), bf16),
            pltpu.VMEM((HID, WIDTH), bf16),
            pltpu.VMEM((4, 7, WIDTH, 128), bf16),
            pltpu.VMEM((4, PIECE, WIDTH), bf16),
            pltpu.VMEM((4, 4 * TOK, WIDTH), bf16),
            pltpu.VMEM((4, RANK, WIDTH), bf16),
            pltpu.VMEM((RANK, HID), bf16),
            pltpu.VMEM((TOK, HID), bf16),
            pltpu.VMEM((TOK, HID), f32),
            pltpu.VMEM((TOK, HID), f32),
            pltpu.VMEM((TOK, HID), f32),
            pltpu.VMEM((4, 7, TOK, 128), bf16),
            pltpu.VMEM((4, 7, TOK, 128), bf16),
            pltpu.VMEM((TOK, RANK), f32),
            pltpu.VMEM((4, TOK, RANK), bf16),
            pltpu.VMEM((4, TOK, RANK), bf16),
            pltpu.VMEM((32, 8, 128), f32),
            pltpu.VMEM((3, 8, 8, 128), f32),
            pltpu.VMEM((8, 8, 128), f32),
            pltpu.VMEM((3, 2, 8, 128), f32),
            pltpu.VMEM((2, 8, 128), f32),
            pltpu.VMEM((8, 128), f32),
            pltpu.SemaphoreType.DMA((COPIES,)),
            pltpu.SemaphoreType.DMA((COPIES,)),
            pltpu.SemaphoreType.DMA((4,)),
            pltpu.SemaphoreType.DMA((4,)),
            pltpu.SemaphoreType.DMA((4,)),
            pltpu.SemaphoreType.DMA((4 * RANKS + 4,)),
            pltpu.SemaphoreType.DMA((4 * RANKS + 4,)),
        ],
        compiler_params=pltpu.CompilerParams(
            collective_id=0, has_side_effects=True, vmem_limit_bytes=60 * 1024 * 1024
        ),
    )(grad_out, gate_act, up_act, down_weight, counts, down_seed, up_seed)


def solution(mesh):
    in_specs = (
        P("col", "row"),
        P("row", "col"),
        P("row", "col"),
        P("col", "row"),
        P("row"),
        P(),
        P(),
    )
    out_specs = (P("row", "col"), P("row", "col"), P("row", "col", None))
    return jax.shard_map(shards, mesh=mesh, in_specs=in_specs, out_specs=out_specs, check_vma=False)
```

```python
import math

import jax
import jax.numpy as jnp
from jax import lax
from jax.experimental import pallas as pl
from jax.experimental.pallas import tpu as pltpu
from jax.sharding import PartitionSpec as P

D = 8192
FF = 28672
RANK = 64
TOK = 128
PIECE = 64
WIDTH = 512
HID = 896
CHUNKS = ((0, 2), (2, 2), (4, 1), (5, 1), (6, 1))
DIRECT = (3, 4)
RANKS = len(CHUNKS)
NT = (((1,), (1,)), ((), ()))
MESH = pl.DeviceIdType.MESH
COPIES = 96


def scramble(values):
    values = values ^ values >> 16 & 65535
    values = values * 73244475
    values = values ^ values >> 16 & 65535
    values = values * 73244475
    return values ^ values >> 16 & 65535


def projection_t(seed_value, first_row, row_count):
    row_number = first_row + lax.broadcasted_iota(jnp.int32, (RANK, row_count), 1)
    rank_number = lax.broadcasted_iota(jnp.int32, (RANK, row_count), 0)
    seed_mix = scramble(seed_value + 40503)
    hashed = scramble(row_number * RANK + rank_number ^ seed_mix)
    return ((hashed >> 8 & 255).astype(jnp.float32) - 127.5).astype(jnp.bfloat16)


def kernel(
    grad_ref, gate_ref, up_ref, weight_ref, counts_ref, down_seed_ref, up_seed_ref,
    gate_out, up_out, feat_out,
    gate_in, up_in, weight_in, weights, zblocks, grads, up_proj, down_proj, hidden,
    gate_factor, up_factor, own, part_out, part_on, part_in, rank_own, rank_out, rank_on, rank_in,
    feat_y, feat_y_in, feat_z, feat_z_in, feat_c, feat_c_in,
    send_sem, recv_sem, local_sem, cross_send, cross_recv, part_send, part_recv,
):
    row = lax.axis_index("row")
    col = lax.axis_index("col")
    x, zl = lax.div(row, 4), lax.rem(row, 4)
    zh, y, c = lax.div(col, 8), lax.rem(lax.div(col, 2), 4), lax.rem(col, 2)

    def turn(value, step):
        return lax.rem(value + step, 4)

    def device(x=x, zl=zl, zh=zh, y=y, c=c):
        return (x * 4 + zl, (zh * 4 + y) * 2 + c)

    sibling = device(c=1 - c)
    started = []

    def send(src, dst, target):
        index = len(started)
        copy = pltpu.make_async_remote_copy(
            src_ref=src, dst_ref=dst, send_sem=send_sem.at[index], recv_sem=recv_sem.at[index],
            device_id=target, device_id_type=MESH,
        )
        copy.start()
        started.append(copy)
        return copy

    locals_ = []
    for number, (src, dst) in enumerate(
        ((weight_ref, weight_in), (gate_ref, gate_in), (up_ref, up_in))
    ):
        copy = pltpu.make_async_copy(src, dst, local_sem.at[number])
        copy.start()
        locals_.append(copy)

    barrier = pltpu.get_barrier_semaphore()
    peers = [sibling]
    for step in (1, 2, 3):
        peers += [
            device(x=turn(x, step)), device(zl=turn(zl, step)),
            device(zh=turn(zh, step)), device(y=turn(y, step)),
        ]
    for peer in peers:
        pl.semaphore_signal(barrier, inc=1, device_id=peer, device_id_type=MESH)

    locals_[0].wait()
    def turn_weight(*pieces):
        for piece in pieces:
            weights[x, piece] = weight_in[piece * 128 : piece * 128 + 128, :].T

    turn_weight(0, 1)
    pl.semaphore_wait(barrier, len(peers))


    def mine(group):
        return pl.ds(pl.multiple_of(group * TOK + c * PIECE, PIECE), PIECE)

    def cross(step, src):
        target = turn(zh, step)
        slot = grads.at[x, mine(y)]
        remote = pltpu.make_async_remote_copy(
            src_ref=src, dst_ref=slot, send_sem=cross_send.at[step], recv_sem=cross_recv.at[x],
            device_id=device(x=target), device_id_type=MESH,
        )
        local = pltpu.make_async_copy(src, slot, local_sem.at[3])

        @pl.when(target != x)
        def _():
            remote.start()

        @pl.when(target == x)
        def _():
            local.start()

        return target, remote

    def send_weight(piece):
        block = weights.at[x, piece]
        right = send(block, block, device(x=turn(x, 1)))
        left = send(block, block, device(x=turn(x, 3)))
        return right, left

    def forward_weight(piece, copies):
        right, left = copies
        right.wait_recv()
        block = weights.at[turn(x, 3), piece, pl.ds(0, WIDTH // 2)]
        on_right = send(block, block, device(x=turn(x, 1)))
        left.wait_recv()
        block = weights.at[turn(x, 1), piece, pl.ds(WIDTH // 2, WIDTH // 2)]
        on_left = send(block, block, device(x=turn(x, 3)))
        return on_right, on_left

    def wait_weights(*pieces):
        for copies in pieces:
            for copy in copies:
                copy.wait_recv()

    z_up = send(grad_ref, zblocks.at[zh], device(zh=turn(zh, 1)))
    z_down = send(grad_ref, zblocks.at[zh], device(zh=turn(zh, 3)))
    crossed = [cross(0, grad_ref)]
    w0 = send_weight(0)
    w1 = send_weight(1)

    turn_weight(2)
    locals_[1].wait()
    locals_[2].wait()
    for part in range(7):
        cols = slice(part * 128, part * 128 + 128)
        gate_value = gate_in[:, cols].astype(jnp.float32)
        up_value = up_in[:, cols].astype(jnp.float32)
        sigmoid_gate = jax.nn.sigmoid(gate_value)
        silu_gate = gate_value * sigmoid_gate
        gate_factor[:, cols] = up_value * sigmoid_gate * (1.0 + gate_value * (1.0 - sigmoid_gate))
        up_factor[:, cols] = silu_gate
        hidden[:, cols] = (silu_gate * up_value).astype(jnp.bfloat16)

    z_up.wait_recv()
    block = zblocks.at[turn(zh, 3), pl.ds(0, 32)]
    z_on_up = send(block, block, device(zh=turn(zh, 1)))
    crossed.append(cross(3, zblocks.at[turn(zh, 3)]))
    z_down.wait_recv()
    block = zblocks.at[turn(zh, 1), pl.ds(32, 32)]
    z_on_down = send(block, block, device(zh=turn(zh, 3)))
    crossed.append(cross(1, zblocks.at[turn(zh, 1)]))

    w0_on = forward_weight(0, w0)
    w1_on = forward_weight(1, w1)
    w2 = send_weight(2)
    turn_weight(3, 4)
    for part in range(4):
        up_proj[part] = projection_t(up_seed_ref[0], (part * 4 + zl) * WIDTH, WIDTH)

    z_on_up.wait_recv()
    z_on_down.wait_recv()
    crossed.append(cross(2, zblocks.at[turn(zh, 2)]))
    w3 = send_weight(3)
    w2_on = forward_weight(2, w2)
    turn_weight(5, 6)
    down_proj[...] = projection_t(down_seed_ref[0], col * HID, HID)
    hidden_ranks = lax.dot_general(
        down_proj[...], hidden[...], NT, preferred_element_type=jnp.float32
    ) * (1.0 / math.sqrt(FF * 5461.25))

    pltpu.make_async_copy(grad_ref, grads.at[x, mine(y)], local_sem.at[3]).wait()
    for step in (1, 2, 3):
        source = turn(x, step)
        slot = grads.at[source, mine(y)]
        pltpu.make_async_remote_copy(
            src_ref=slot, dst_ref=slot, send_sem=cross_send.at[step], recv_sem=cross_recv.at[source],
            device_id=device(x=source), device_id_type=MESH,
        ).wait_recv()

    def y_block(source, first=0, count=4):
        return grads.at[pl.ds(first, count), mine(source)]

    side, inner = lax.div(zl, 2), lax.rem(zl + lax.div(zl, 2), 2) == 1
    mate = side * 2 + 1 - lax.rem(zl, 2)

    def is_across(target):
        return lax.div(target, 2) != side

    def part_copy(chunk, kind, target, source=None):
        if chunk == RANKS:
            at = ()
        else:
            at = (pl.ds(*CHUNKS[chunk]),)
        src = (rank_out if chunk == RANKS else part_out).at[(target,) + at]
        if kind == 1:
            slot = lax.rem(target, 2)
            dst = (rank_on if chunk == RANKS else part_on).at[(slot,) + at]
            sem = 2 + slot
        else:
            slot = 0 if kind == 0 else 1
            if kind == 2 and chunk in DIRECT:
                slot = 1 + lax.rem(zl, 2) if source is None else source
            dst = (rank_in if chunk == RANKS else part_in).at[(slot,) + at]
            sem = slot
        return pltpu.make_async_remote_copy(
            src_ref=src, dst_ref=dst, send_sem=part_send.at[chunk * 4 + target],
            recv_sem=part_recv.at[chunk * 4 + sem],
            device_id=device(zl=target if kind == 2 else mate), device_id_type=MESH,
        )

    def wait_parts(chunk):
        part_copy(chunk, 0, mate).wait_recv()
        part_copy(chunk, 2, lax.rem(zl + 2, 4), 1).wait_recv()
        if chunk in DIRECT:
            part_copy(chunk, 2, lax.rem(zl + 2, 4), 2).wait_recv()

    def put(chunk, target, total):
        if chunk == RANKS:
            rank_out[target] = total.astype(jnp.bfloat16)
        else:
            first, count = CHUNKS[chunk]
            for lane in range(count):
                part_out[target, first + lane] = total[:, lane * 128 : lane * 128 + 128].astype(
                    jnp.bfloat16
                )

    pending = []

    def multiply(chunk, target):
        tokens = pl.ds(pl.multiple_of(target * TOK, TOK), TOK)
        total = None
        for part in range(4):
            left = grads[part, tokens]
            if chunk == RANKS:
                product = lax.dot_general(
                    left, up_proj[part], NT, preferred_element_type=jnp.float32
                )
            else:
                first, count = CHUNKS[chunk]
                right = [weights[part, first + piece] for piece in range(count)]
                right = jnp.concatenate(right, axis=1) if count > 1 else right[0]
                product = jnp.dot(left, right, preferred_element_type=jnp.float32)
            total = product if part == 0 else total + product

        keep = target == zl
        if chunk not in DIRECT:
            keep |= is_across(target) & inner

        @pl.when(keep)
        def _():
            if chunk == RANKS:
                rank_own[target] = total
            else:
                own[target, :, first * 128 : (first + count) * 128] = total

        @pl.when(target == mate)
        def _():
            put(chunk, target, total)
            part_copy(chunk, 0, target).start()

        if chunk in DIRECT:

            @pl.when(is_across(target))
            def _():
                put(chunk, target, total)
                part_copy(chunk, 2, target).start()

        else:

            @pl.when(is_across(target) & jnp.logical_not(inner))
            def _():
                put(chunk, target, total)
                part_copy(chunk, 1, target).start()

            pending.append((chunk, target))

    def relay(most=0):
        while len(pending) > most:
            chunk, target = pending.pop(0)

            @pl.when(is_across(target) & inner)
            def _(chunk=chunk, target=target):
                part_copy(chunk, 1, target).wait_recv()
                slot = lax.rem(target, 2)
                if chunk == RANKS:
                    put(chunk, target, rank_own[target] + rank_on[slot].astype(jnp.float32))
                else:
                    first, count = CHUNKS[chunk]
                    for lane in range(first, first + count):
                        part_out[target, lane] = (
                            own[target, :, lane * 128 : lane * 128 + 128]
                            + part_on[slot, lane].astype(jnp.float32)
                        ).astype(jnp.bfloat16)
                part_copy(chunk, 2, target).start()

    def multiply_all(chunk):
        for target in (2 - side * 2, 3 - side * 2, mate, zl):
            multiply(chunk, target)

    def finish(chunk):
        wait_parts(chunk)
        first, count = CHUNKS[chunk]
        for lane in range(first, first + count):
            cols = slice(lane * 128, lane * 128 + 128)
            total = own[zl, :, cols]
            for source in range(3 if chunk in DIRECT else 2):
                total += part_in[source, lane].astype(jnp.float32)
            gate_out[:, cols] = (total * gate_factor[:, cols]).astype(jnp.bfloat16)
            up_out[:, cols] = (total * up_factor[:, cols]).astype(jnp.bfloat16)

    block = y_block(y)
    y_up = send(block, block, device(y=turn(y, 1)))
    y_down = send(block, block, device(y=turn(y, 3)))
    across = [send(block, block, sibling)]
    w4 = send_weight(4)
    w3_on = forward_weight(3, w3)

    across[0].wait_recv()
    multiply(RANKS, turn(y, 0))
    wait_weights(w0_on, w1_on)
    multiply(0, turn(y, 0))
    w5 = send_weight(5)

    relay()
    y_up.wait_recv()
    block = y_block(turn(y, 3), 0, 2)
    y_on_up = send(block, block, device(y=turn(y, 1)))
    block = y_block(turn(y, 3))
    across.append(send(block, block, sibling))
    y_down.wait_recv()
    block = y_block(turn(y, 1), 2, 2)
    y_on_down = send(block, block, device(y=turn(y, 3)))
    block = y_block(turn(y, 1))
    across.append(send(block, block, sibling))
    wait_weights(w2_on, w3_on)
    multiply(1, turn(y, 0))
    relay()
    w4_on = forward_weight(4, w4)
    w6 = send_weight(6)

    for place, step in ((1, 3), (2, 1)):
        across[place].wait_recv()
        multiply(RANKS, turn(y, step))
        multiply(0, turn(y, step))
        relay(2)
    y_on_up.wait_recv()
    block = y_block(turn(y, 2), 0, 2)
    across.append(send(block, block, sibling))
    y_on_down.wait_recv()
    block = y_block(turn(y, 2), 2, 2)
    across.append(send(block, block, sibling))
    multiply(1, turn(y, 3))
    multiply(1, turn(y, 1))
    relay()
    w5_on = forward_weight(5, w5)

    across[3].wait_recv()
    across[4].wait_recv()
    multiply(RANKS, turn(y, 2))
    multiply(0, turn(y, 2))
    relay(2)
    multiply(1, turn(y, 2))
    wait_weights(w4_on)
    multiply_all(2)
    relay()
    w6_on = forward_weight(6, w6)

    wait_parts(RANKS)
    grad_ranks = rank_own[zl]
    for source in range(2):
        grad_ranks += rank_in[source].astype(jnp.float32)
    grad_ranks *= 1.0 / math.sqrt(D * 5461.25)
    live_count = counts_ref[0]
    positions = lax.broadcasted_iota(jnp.int32, (RANK, TOK), 1)
    masked = hidden_ranks * jnp.where(positions < live_count, 1.0, 0.0)
    features = jnp.dot(
        masked, grad_ranks, precision=lax.Precision.HIGHEST, preferred_element_type=jnp.float32
    )
    feat_y[...] = jnp.zeros_like(feat_y)
    for owner in range(32):
        slot = owner // 2 % 4 * 8 + owner // 8 * 2 + owner % 2
        feat_y[slot, 0:2, 0:RANK] = features[owner * 2 : owner * 2 + 2, :]
    y_copies = [
        send(
            feat_y.at[pl.ds(turn(y, step) * 8, 8)], feat_y_in.at[step - 1],
            device(y=turn(y, step)),
        )
        for step in (1, 2, 3)
    ]

    wait_weights(w5_on)
    multiply_all(3)
    relay()
    for copy in y_copies:
        copy.wait_recv()
    feat_z[...] = feat_y[pl.ds(y * 8, 8)] + feat_y_in[0] + feat_y_in[1] + feat_y_in[2]
    z_copies = [
        send(
            feat_z.at[pl.ds(turn(zh, step) * 2, 2)], feat_z_in.at[step - 1],
            device(zh=turn(zh, step)),
        )
        for step in (1, 2, 3)
    ]
    finish(0)

    wait_weights(w6_on)
    multiply_all(4)
    relay()
    finish(1)
    for copy in z_copies:
        copy.wait_recv()
    feat_c[...] = feat_z[pl.ds(zh * 2, 2)] + feat_z_in[0] + feat_z_in[1] + feat_z_in[2]
    c_copy = send(feat_c.at[1 - c], feat_c_in, sibling)
    finish(2)
    c_copy.wait_recv()
    counted = jnp.full((8, 128), live_count, jnp.int32).astype(jnp.float32)
    result = (feat_c[c] + feat_c_in[...]) * lax.rsqrt(counted)
    feat_out[0] = result[0:2, 0:RANK]
    finish(3)
    finish(4)

    for chunk in range(RANKS + 1):
        for target in range(4):

            @pl.when(zl != target)
            def _(chunk=chunk, target=target):
                part_copy(chunk, 2, target).wait_send()

    for copy in started:
        copy.wait_send()
    for target, remote in crossed:

        @pl.when(target != x)
        def _(remote=remote):
            remote.wait_send()


def shards(grad_out, gate_act, up_act, down_weight, counts, down_seed, up_seed):
    hbm = pl.BlockSpec(memory_space=pltpu.HBM)
    smem = pl.BlockSpec(memory_space=pltpu.SMEM)
    vmem = pl.BlockSpec(memory_space=pltpu.VMEM)
    bf16, f32 = jnp.bfloat16, jnp.float32
    return pl.pallas_call(
        kernel,
        out_shape=(
            pltpu.VMEM((TOK, HID), bf16),
            pltpu.VMEM((TOK, HID), bf16),
            pltpu.VMEM((1, 2, RANK), f32),
        ),
        in_specs=[hbm, hbm, hbm, hbm, smem, smem, smem],
        out_specs=(vmem, vmem, vmem),
        scratch_shapes=[
            pltpu.VMEM((TOK, HID), bf16),
            pltpu.VMEM((TOK, HID), bf16),
            pltpu.VMEM((HID, WIDTH), bf16),
            pltpu.VMEM((4, 7, WIDTH, 128), bf16),
            pltpu.VMEM((4, PIECE, WIDTH), bf16),
            pltpu.VMEM((4, 4 * TOK, WIDTH), bf16),
            pltpu.VMEM((4, RANK, WIDTH), bf16),
            pltpu.VMEM((RANK, HID), bf16),
            pltpu.VMEM((TOK, HID), bf16),
            pltpu.VMEM((TOK, HID), f32),
            pltpu.VMEM((TOK, HID), f32),
            pltpu.VMEM((4, TOK, HID), f32),
            pltpu.VMEM((4, 7, TOK, 128), bf16),
            pltpu.VMEM((2, 7, TOK, 128), bf16),
            pltpu.VMEM((3, 7, TOK, 128), bf16),
            pltpu.VMEM((4, TOK, RANK), f32),
            pltpu.VMEM((4, TOK, RANK), bf16),
            pltpu.VMEM((2, TOK, RANK), bf16),
            pltpu.VMEM((2, TOK, RANK), bf16),
            pltpu.VMEM((32, 8, 128), f32),
            pltpu.VMEM((3, 8, 8, 128), f32),
            pltpu.VMEM((8, 8, 128), f32),
            pltpu.VMEM((3, 2, 8, 128), f32),
            pltpu.VMEM((2, 8, 128), f32),
            pltpu.VMEM((8, 128), f32),
            pltpu.SemaphoreType.DMA((COPIES,)),
            pltpu.SemaphoreType.DMA((COPIES,)),
            pltpu.SemaphoreType.DMA((4,)),
            pltpu.SemaphoreType.DMA((4,)),
            pltpu.SemaphoreType.DMA((4,)),
            pltpu.SemaphoreType.DMA((4 * RANKS + 4,)),
            pltpu.SemaphoreType.DMA((4 * RANKS + 4,)),
        ],
        compiler_params=pltpu.CompilerParams(
            collective_id=0, has_side_effects=True, vmem_limit_bytes=60 * 1024 * 1024
        ),
    )(grad_out, gate_act, up_act, down_weight, counts, down_seed, up_seed)


def solution(mesh):
    in_specs = (
        P("col", "row"),
        P("row", "col"),
        P("row", "col"),
        P("col", "row"),
        P("row"),
        P(),
        P(),
    )
    out_specs = (P("row", "col"), P("row", "col"), P("row", "col", None))
    return jax.shard_map(shards, mesh=mesh, in_specs=in_specs, out_specs=out_specs, check_vma=False)
```

```python
import math

import jax
import jax.numpy as jnp
from jax import lax
from jax.experimental import pallas as pl
from jax.experimental.pallas import tpu as pltpu
from jax.sharding import PartitionSpec as P

D = 8192
FF = 28672
RANK = 64
TOK = 128
PIECE = 64
WIDTH = 512
HID = 896
CHUNKS = ((0, 2), (2, 2), (4, 1), (5, 1), (6, 1))
DIRECT = (3, 4)
RANKS = len(CHUNKS)
NT = (((1,), (1,)), ((), ()))
MESH = pl.DeviceIdType.MESH
COPIES = 96


def scramble(values):
    values = values ^ values >> 16 & 65535
    values = values * 73244475
    values = values ^ values >> 16 & 65535
    values = values * 73244475
    return values ^ values >> 16 & 65535


def projection_t(seed_value, first_row, row_count):
    row_number = first_row + lax.broadcasted_iota(jnp.int32, (RANK, row_count), 1)
    rank_number = lax.broadcasted_iota(jnp.int32, (RANK, row_count), 0)
    seed_mix = scramble(seed_value + 40503)
    hashed = scramble(row_number * RANK + rank_number ^ seed_mix)
    return ((hashed >> 8 & 255).astype(jnp.float32) - 127.5).astype(jnp.bfloat16)


def kernel(
    grad_ref, gate_ref, up_ref, weight_ref, counts_ref, down_seed_ref, up_seed_ref,
    gate_out, up_out, feat_out,
    gate_in, up_in, weight_in, weights, zblocks, grads, up_proj, down_proj, hidden,
    gate_factor, up_factor, own, part_out, part_on, part_in, rank_own, rank_out, rank_on, rank_in,
    feat_y, feat_y_in, feat_z, feat_z_in, feat_c, feat_c_in,
    send_sem, recv_sem, local_sem, cross_send, cross_recv, part_send, part_recv,
):
    row = lax.axis_index("row")
    col = lax.axis_index("col")
    x, zl = lax.div(row, 4), lax.rem(row, 4)
    zh, y, c = lax.div(col, 8), lax.rem(lax.div(col, 2), 4), lax.rem(col, 2)

    def turn(value, step):
        return lax.rem(value + step, 4)

    def device(x=x, zl=zl, zh=zh, y=y, c=c):
        return (x * 4 + zl, (zh * 4 + y) * 2 + c)

    sibling = device(c=1 - c)
    started = []

    def send(src, dst, target):
        index = len(started)
        copy = pltpu.make_async_remote_copy(
            src_ref=src, dst_ref=dst, send_sem=send_sem.at[index], recv_sem=recv_sem.at[index],
            device_id=target, device_id_type=MESH,
        )
        copy.start()
        started.append(copy)
        return copy

    locals_ = []
    for number, (src, dst) in enumerate(
        ((weight_ref, weight_in), (gate_ref, gate_in), (up_ref, up_in))
    ):
        copy = pltpu.make_async_copy(src, dst, local_sem.at[number])
        copy.start()
        locals_.append(copy)

    barrier = pltpu.get_barrier_semaphore()
    peers = [sibling]
    for step in (1, 2, 3):
        peers += [
            device(x=turn(x, step)), device(zl=turn(zl, step)),
            device(zh=turn(zh, step)), device(y=turn(y, step)),
        ]
    for peer in peers:
        pl.semaphore_signal(barrier, inc=1, device_id=peer, device_id_type=MESH)

    locals_[0].wait()
    def turn_weight(*pieces):
        for piece in pieces:
            weights[x, piece] = weight_in[piece * 128 : piece * 128 + 128, :].T

    turn_weight(0, 1)
    pl.semaphore_wait(barrier, len(peers))


    def mine(group):
        return pl.ds(pl.multiple_of(group * TOK + c * PIECE, PIECE), PIECE)

    def cross(step, src):
        target = turn(zh, step)
        slot = grads.at[x, mine(y)]
        remote = pltpu.make_async_remote_copy(
            src_ref=src, dst_ref=slot, send_sem=cross_send.at[step], recv_sem=cross_recv.at[x],
            device_id=device(x=target), device_id_type=MESH,
        )
        local = pltpu.make_async_copy(src, slot, local_sem.at[3])

        @pl.when(target != x)
        def _():
            remote.start()

        @pl.when(target == x)
        def _():
            local.start()

        return target, remote

    def send_weight(piece):
        block = weights.at[x, piece]
        right = send(block, block, device(x=turn(x, 1)))
        left = send(block, block, device(x=turn(x, 3)))
        return right, left

    def forward_weight(piece, copies):
        right, left = copies
        right.wait_recv()
        block = weights.at[turn(x, 3), piece, pl.ds(0, WIDTH // 2)]
        on_right = send(block, block, device(x=turn(x, 1)))
        left.wait_recv()
        block = weights.at[turn(x, 1), piece, pl.ds(WIDTH // 2, WIDTH // 2)]
        on_left = send(block, block, device(x=turn(x, 3)))
        return on_right, on_left

    def wait_weights(*pieces):
        for copies in pieces:
            for copy in copies:
                copy.wait_recv()

    z_up = send(grad_ref, zblocks.at[zh], device(zh=turn(zh, 1)))
    z_down = send(grad_ref, zblocks.at[zh], device(zh=turn(zh, 3)))
    crossed = [cross(0, grad_ref)]
    w0 = send_weight(0)
    w1 = send_weight(1)

    turn_weight(2)
    locals_[1].wait()
    locals_[2].wait()
    for part in range(7):
        cols = slice(part * 128, part * 128 + 128)
        gate_value = gate_in[:, cols].astype(jnp.float32)
        up_value = up_in[:, cols].astype(jnp.float32)
        sigmoid_gate = jax.nn.sigmoid(gate_value)
        silu_gate = gate_value * sigmoid_gate
        gate_factor[:, cols] = up_value * sigmoid_gate * (1.0 + gate_value * (1.0 - sigmoid_gate))
        up_factor[:, cols] = silu_gate
        hidden[:, cols] = (silu_gate * up_value).astype(jnp.bfloat16)

    z_up.wait_recv()
    block = zblocks.at[turn(zh, 3), pl.ds(0, 32)]
    z_on_up = send(block, block, device(zh=turn(zh, 1)))
    crossed.append(cross(3, zblocks.at[turn(zh, 3)]))
    z_down.wait_recv()
    block = zblocks.at[turn(zh, 1), pl.ds(32, 32)]
    z_on_down = send(block, block, device(zh=turn(zh, 3)))
    crossed.append(cross(1, zblocks.at[turn(zh, 1)]))

    w0_on = forward_weight(0, w0)
    w1_on = forward_weight(1, w1)
    w2 = send_weight(2)
    turn_weight(3, 4)
    for part in range(4):
        up_proj[part] = projection_t(up_seed_ref[0], (part * 4 + zl) * WIDTH, WIDTH)

    z_on_up.wait_recv()
    z_on_down.wait_recv()
    crossed.append(cross(2, zblocks.at[turn(zh, 2)]))
    w3 = send_weight(3)
    w2_on = forward_weight(2, w2)
    turn_weight(5, 6)
    down_proj[...] = projection_t(down_seed_ref[0], col * HID, HID)
    hidden_ranks = lax.dot_general(
        down_proj[...], hidden[...], NT, preferred_element_type=jnp.float32
    ) * (1.0 / math.sqrt(FF * 5461.25))

    pltpu.make_async_copy(grad_ref, grads.at[x, mine(y)], local_sem.at[3]).wait()
    for step in (1, 2, 3):
        source = turn(x, step)
        slot = grads.at[source, mine(y)]
        pltpu.make_async_remote_copy(
            src_ref=slot, dst_ref=slot, send_sem=cross_send.at[step], recv_sem=cross_recv.at[source],
            device_id=device(x=source), device_id_type=MESH,
        ).wait_recv()

    def y_block(source, first=0, count=4):
        return grads.at[pl.ds(first, count), mine(source)]

    side, inner = lax.div(zl, 2), lax.rem(zl + lax.div(zl, 2), 2) == 1
    mate = side * 2 + 1 - lax.rem(zl, 2)

    def is_across(target):
        return lax.div(target, 2) != side

    def part_copy(chunk, kind, target, source=None):
        if chunk == RANKS:
            at = ()
        else:
            at = (pl.ds(*CHUNKS[chunk]),)
        src = (rank_out if chunk == RANKS else part_out).at[(target,) + at]
        if kind == 1:
            slot = lax.rem(target, 2)
            dst = (rank_on if chunk == RANKS else part_on).at[(slot,) + at]
            sem = 2 + slot
        else:
            slot = 0 if kind == 0 else 1
            if kind == 2 and chunk in DIRECT:
                slot = 1 + lax.rem(zl, 2) if source is None else source
            dst = (rank_in if chunk == RANKS else part_in).at[(slot,) + at]
            sem = slot
        return pltpu.make_async_remote_copy(
            src_ref=src, dst_ref=dst, send_sem=part_send.at[chunk * 4 + target],
            recv_sem=part_recv.at[chunk * 4 + sem],
            device_id=device(zl=target if kind == 2 else mate), device_id_type=MESH,
        )

    def wait_parts(chunk):
        part_copy(chunk, 0, mate).wait_recv()
        part_copy(chunk, 2, lax.rem(zl + 2, 4), 1).wait_recv()
        if chunk in DIRECT:
            part_copy(chunk, 2, lax.rem(zl + 2, 4), 2).wait_recv()

    def put(chunk, target, total):
        if chunk == RANKS:
            rank_out[target] = total.astype(jnp.bfloat16)
        else:
            first, count = CHUNKS[chunk]
            for lane in range(count):
                part_out[target, first + lane] = total[:, lane * 128 : lane * 128 + 128].astype(
                    jnp.bfloat16
                )

    pending = []

    def multiply(chunk, target):
        tokens = pl.ds(pl.multiple_of(target * TOK, TOK), TOK)
        total = None
        for part in range(4):
            left = grads[part, tokens]
            if chunk == RANKS:
                product = lax.dot_general(
                    left, up_proj[part], NT, preferred_element_type=jnp.float32
                )
            else:
                first, count = CHUNKS[chunk]
                right = [weights[part, first + piece] for piece in range(count)]
                right = jnp.concatenate(right, axis=1) if count > 1 else right[0]
                product = jnp.dot(left, right, preferred_element_type=jnp.float32)
            total = product if part == 0 else total + product

        keep = target == zl
        if chunk not in DIRECT:
            keep |= is_across(target) & inner

        @pl.when(keep)
        def _():
            if chunk == RANKS:
                rank_own[target] = total
            else:
                own[target, :, first * 128 : (first + count) * 128] = total

        @pl.when(target == mate)
        def _():
            put(chunk, target, total)
            part_copy(chunk, 0, target).start()

        if chunk in DIRECT:

            @pl.when(is_across(target))
            def _():
                put(chunk, target, total)
                part_copy(chunk, 2, target).start()

        else:

            @pl.when(is_across(target) & jnp.logical_not(inner))
            def _():
                put(chunk, target, total)
                part_copy(chunk, 1, target).start()

            pending.append((chunk, target))

    def relay(most=0):
        while len(pending) > most:
            chunk, target = pending.pop(0)

            @pl.when(is_across(target) & inner)
            def _(chunk=chunk, target=target):
                part_copy(chunk, 1, target).wait_recv()
                slot = lax.rem(target, 2)
                if chunk == RANKS:
                    put(chunk, target, rank_own[target] + rank_on[slot].astype(jnp.float32))
                else:
                    first, count = CHUNKS[chunk]
                    for lane in range(first, first + count):
                        part_out[target, lane] = (
                            own[target, :, lane * 128 : lane * 128 + 128]
                            + part_on[slot, lane].astype(jnp.float32)
                        ).astype(jnp.bfloat16)
                part_copy(chunk, 2, target).start()

    def multiply_all(chunk):
        for target in (2 - side * 2, 3 - side * 2, mate, zl):
            multiply(chunk, target)

    def finish(chunk):
        wait_parts(chunk)
        first, count = CHUNKS[chunk]
        for lane in range(first, first + count):
            cols = slice(lane * 128, lane * 128 + 128)
            total = own[zl, :, cols]
            for source in range(3 if chunk in DIRECT else 2):
                total += part_in[source, lane].astype(jnp.float32)
            gate_out[:, cols] = (total * gate_factor[:, cols]).astype(jnp.bfloat16)
            up_out[:, cols] = (total * up_factor[:, cols]).astype(jnp.bfloat16)

    block = y_block(y)
    y_up = send(block, block, device(y=turn(y, 1)))
    y_down = send(block, block, device(y=turn(y, 3)))
    across = [send(block, block, sibling)]
    w4 = send_weight(4)
    w3_on = forward_weight(3, w3)
    w5 = send_weight(5)

    across[0].wait_recv()
    multiply(RANKS, turn(y, 0))
    wait_weights(w0_on, w1_on)
    multiply(0, turn(y, 0))

    relay()
    y_up.wait_recv()
    block = y_block(turn(y, 3), 0, 2)
    y_on_up = send(block, block, device(y=turn(y, 1)))
    block = y_block(turn(y, 3))
    across.append(send(block, block, sibling))
    y_down.wait_recv()
    block = y_block(turn(y, 1), 2, 2)
    y_on_down = send(block, block, device(y=turn(y, 3)))
    block = y_block(turn(y, 1))
    across.append(send(block, block, sibling))
    w6 = send_weight(6)
    w4_on = forward_weight(4, w4)
    wait_weights(w2_on, w3_on)
    multiply(1, turn(y, 0))
    relay()

    for place, step in ((1, 3), (2, 1)):
        across[place].wait_recv()
        multiply(RANKS, turn(y, step))
        multiply(0, turn(y, step))
        relay(2)
    y_on_up.wait_recv()
    block = y_block(turn(y, 2), 0, 2)
    across.append(send(block, block, sibling))
    y_on_down.wait_recv()
    block = y_block(turn(y, 2), 2, 2)
    across.append(send(block, block, sibling))
    multiply(1, turn(y, 3))
    multiply(1, turn(y, 1))
    relay()
    w5_on = forward_weight(5, w5)

    across[3].wait_recv()
    across[4].wait_recv()
    multiply(RANKS, turn(y, 2))
    multiply(0, turn(y, 2))
    relay(2)
    multiply(1, turn(y, 2))
    wait_weights(w4_on)
    multiply_all(2)
    relay()
    w6_on = forward_weight(6, w6)

    wait_parts(RANKS)
    grad_ranks = rank_own[zl]
    for source in range(2):
        grad_ranks += rank_in[source].astype(jnp.float32)
    grad_ranks *= 1.0 / math.sqrt(D * 5461.25)
    live_count = counts_ref[0]
    positions = lax.broadcasted_iota(jnp.int32, (RANK, TOK), 1)
    masked = hidden_ranks * jnp.where(positions < live_count, 1.0, 0.0)
    features = jnp.dot(
        masked, grad_ranks, precision=lax.Precision.HIGHEST, preferred_element_type=jnp.float32
    )
    feat_y[...] = jnp.zeros_like(feat_y)
    for owner in range(32):
        slot = owner // 2 % 4 * 8 + owner // 8 * 2 + owner % 2
        feat_y[slot, 0:2, 0:RANK] = features[owner * 2 : owner * 2 + 2, :]
    y_copies = [
        send(
            feat_y.at[pl.ds(turn(y, step) * 8, 8)], feat_y_in.at[step - 1],
            device(y=turn(y, step)),
        )
        for step in (1, 2, 3)
    ]

    wait_weights(w5_on)
    multiply_all(3)
    relay()
    for copy in y_copies:
        copy.wait_recv()
    feat_z[...] = feat_y[pl.ds(y * 8, 8)] + feat_y_in[0] + feat_y_in[1] + feat_y_in[2]
    z_copies = [
        send(
            feat_z.at[pl.ds(turn(zh, step) * 2, 2)], feat_z_in.at[step - 1],
            device(zh=turn(zh, step)),
        )
        for step in (1, 2, 3)
    ]
    finish(0)

    wait_weights(w6_on)
    multiply_all(4)
    relay()
    finish(1)
    for copy in z_copies:
        copy.wait_recv()
    feat_c[...] = feat_z[pl.ds(zh * 2, 2)] + feat_z_in[0] + feat_z_in[1] + feat_z_in[2]
    c_copy = send(feat_c.at[1 - c], feat_c_in, sibling)
    finish(2)
    c_copy.wait_recv()
    counted = jnp.full((8, 128), live_count, jnp.int32).astype(jnp.float32)
    result = (feat_c[c] + feat_c_in[...]) * lax.rsqrt(counted)
    feat_out[0] = result[0:2, 0:RANK]
    finish(3)
    finish(4)

    for chunk in range(RANKS + 1):
        for target in range(4):

            @pl.when(zl != target)
            def _(chunk=chunk, target=target):
                part_copy(chunk, 2, target).wait_send()

    for copy in started:
        copy.wait_send()
    for target, remote in crossed:

        @pl.when(target != x)
        def _(remote=remote):
            remote.wait_send()


def shards(grad_out, gate_act, up_act, down_weight, counts, down_seed, up_seed):
    hbm = pl.BlockSpec(memory_space=pltpu.HBM)
    smem = pl.BlockSpec(memory_space=pltpu.SMEM)
    vmem = pl.BlockSpec(memory_space=pltpu.VMEM)
    bf16, f32 = jnp.bfloat16, jnp.float32
    return pl.pallas_call(
        kernel,
        out_shape=(
            pltpu.VMEM((TOK, HID), bf16),
            pltpu.VMEM((TOK, HID), bf16),
            pltpu.VMEM((1, 2, RANK), f32),
        ),
        in_specs=[hbm, hbm, hbm, hbm, smem, smem, smem],
        out_specs=(vmem, vmem, vmem),
        scratch_shapes=[
            pltpu.VMEM((TOK, HID), bf16),
            pltpu.VMEM((TOK, HID), bf16),
            pltpu.VMEM((HID, WIDTH), bf16),
            pltpu.VMEM((4, 7, WIDTH, 128), bf16),
            pltpu.VMEM((4, PIECE, WIDTH), bf16),
            pltpu.VMEM((4, 4 * TOK, WIDTH), bf16),
            pltpu.VMEM((4, RANK, WIDTH), bf16),
            pltpu.VMEM((RANK, HID), bf16),
            pltpu.VMEM((TOK, HID), bf16),
            pltpu.VMEM((TOK, HID), f32),
            pltpu.VMEM((TOK, HID), f32),
            pltpu.VMEM((4, TOK, HID), f32),
            pltpu.VMEM((4, 7, TOK, 128), bf16),
            pltpu.VMEM((2, 7, TOK, 128), bf16),
            pltpu.VMEM((3, 7, TOK, 128), bf16),
            pltpu.VMEM((4, TOK, RANK), f32),
            pltpu.VMEM((4, TOK, RANK), bf16),
            pltpu.VMEM((2, TOK, RANK), bf16),
            pltpu.VMEM((2, TOK, RANK), bf16),
            pltpu.VMEM((32, 8, 128), f32),
            pltpu.VMEM((3, 8, 8, 128), f32),
            pltpu.VMEM((8, 8, 128), f32),
            pltpu.VMEM((3, 2, 8, 128), f32),
            pltpu.VMEM((2, 8, 128), f32),
            pltpu.VMEM((8, 128), f32),
            pltpu.SemaphoreType.DMA((COPIES,)),
            pltpu.SemaphoreType.DMA((COPIES,)),
            pltpu.SemaphoreType.DMA((4,)),
            pltpu.SemaphoreType.DMA((4,)),
            pltpu.SemaphoreType.DMA((4,)),
            pltpu.SemaphoreType.DMA((4 * RANKS + 4,)),
            pltpu.SemaphoreType.DMA((4 * RANKS + 4,)),
        ],
        compiler_params=pltpu.CompilerParams(
            collective_id=0, has_side_effects=True, vmem_limit_bytes=60 * 1024 * 1024
        ),
    )(grad_out, gate_act, up_act, down_weight, counts, down_seed, up_seed)


def solution(mesh):
    in_specs = (
        P("col", "row"),
        P("row", "col"),
        P("row", "col"),
        P("col", "row"),
        P("row"),
        P(),
        P(),
    )
    out_specs = (P("row", "col"), P("row", "col"), P("row", "col", None))
    return jax.shard_map(shards, mesh=mesh, in_specs=in_specs, out_specs=out_specs, check_vma=False)
```

```python
import math

import jax
import jax.numpy as jnp
from jax import lax
from jax.experimental import pallas as pl
from jax.experimental.pallas import tpu as pltpu
from jax.sharding import PartitionSpec as P

D = 8192
FF = 28672
RANK = 64
TOK = 128
PIECE = 64
WIDTH = 512
HID = 896
CHUNKS = ((0, 2), (2, 2), (4, 1), (5, 1), (6, 1))
DIRECT = (3, 4)
RANKS = len(CHUNKS)
NT = (((1,), (1,)), ((), ()))
MESH = pl.DeviceIdType.MESH
COPIES = 96


def scramble(values):
    values = values ^ values >> 16 & 65535
    values = values * 73244475
    values = values ^ values >> 16 & 65535
    values = values * 73244475
    return values ^ values >> 16 & 65535


def projection_t(seed_value, first_row, row_count):
    row_number = first_row + lax.broadcasted_iota(jnp.int32, (RANK, row_count), 1)
    rank_number = lax.broadcasted_iota(jnp.int32, (RANK, row_count), 0)
    seed_mix = scramble(seed_value + 40503)
    hashed = scramble(row_number * RANK + rank_number ^ seed_mix)
    return ((hashed >> 8 & 255).astype(jnp.float32) - 127.5).astype(jnp.bfloat16)


def kernel(
    grad_ref, gate_ref, up_ref, weight_ref, counts_ref, down_seed_ref, up_seed_ref,
    gate_out, up_out, feat_out,
    gate_in, up_in, weight_in, weights, zblocks, grads, up_proj, down_proj, hidden,
    gate_factor, up_factor, own, part_out, part_on, part_in, rank_own, rank_out, rank_on, rank_in,
    feat_y, feat_y_in, feat_z, feat_z_in, feat_c, feat_c_in,
    send_sem, recv_sem, local_sem, cross_send, cross_recv, part_send, part_recv,
):
    row = lax.axis_index("row")
    col = lax.axis_index("col")
    x, zl = lax.div(row, 4), lax.rem(row, 4)
    zh, y, c = lax.div(col, 8), lax.rem(lax.div(col, 2), 4), lax.rem(col, 2)

    def turn(value, step):
        return lax.rem(value + step, 4)

    def device(x=x, zl=zl, zh=zh, y=y, c=c):
        return (x * 4 + zl, (zh * 4 + y) * 2 + c)

    sibling = device(c=1 - c)
    started = []

    def send(src, dst, target):
        index = len(started)
        copy = pltpu.make_async_remote_copy(
            src_ref=src, dst_ref=dst, send_sem=send_sem.at[index], recv_sem=recv_sem.at[index],
            device_id=target, device_id_type=MESH,
        )
        copy.start()
        started.append(copy)
        return copy

    locals_ = []
    for number, (src, dst) in enumerate(
        ((weight_ref, weight_in), (gate_ref, gate_in), (up_ref, up_in))
    ):
        copy = pltpu.make_async_copy(src, dst, local_sem.at[number])
        copy.start()
        locals_.append(copy)

    barrier = pltpu.get_barrier_semaphore()
    peers = [sibling]
    for step in (1, 2, 3):
        peers += [
            device(x=turn(x, step)), device(zl=turn(zl, step)),
            device(zh=turn(zh, step)), device(y=turn(y, step)),
        ]
    for peer in peers:
        pl.semaphore_signal(barrier, inc=1, device_id=peer, device_id_type=MESH)

    locals_[0].wait()
    def turn_weight(*pieces):
        for piece in pieces:
            weights[x, piece] = weight_in[piece * 128 : piece * 128 + 128, :].T

    turn_weight(0, 1)
    pl.semaphore_wait(barrier, len(peers))


    def mine(group):
        return pl.ds(pl.multiple_of(group * TOK + c * PIECE, PIECE), PIECE)

    def cross(step, src):
        target = turn(zh, step)
        slot = grads.at[x, mine(y)]
        remote = pltpu.make_async_remote_copy(
            src_ref=src, dst_ref=slot, send_sem=cross_send.at[step], recv_sem=cross_recv.at[x],
            device_id=device(x=target), device_id_type=MESH,
        )
        local = pltpu.make_async_copy(src, slot, local_sem.at[3])

        @pl.when(target != x)
        def _():
            remote.start()

        @pl.when(target == x)
        def _():
            local.start()

        return target, remote

    def send_weight(piece):
        block = weights.at[x, piece]
        right = send(block, block, device(x=turn(x, 1)))
        left = send(block, block, device(x=turn(x, 3)))
        return right, left

    def forward_weight(piece, copies):
        right, left = copies
        right.wait_recv()
        block = weights.at[turn(x, 3), piece, pl.ds(0, WIDTH // 2)]
        on_right = send(block, block, device(x=turn(x, 1)))
        left.wait_recv()
        block = weights.at[turn(x, 1), piece, pl.ds(WIDTH // 2, WIDTH // 2)]
        on_left = send(block, block, device(x=turn(x, 3)))
        return on_right, on_left

    def wait_weights(*pieces):
        for copies in pieces:
            for copy in copies:
                copy.wait_recv()

    z_up = send(grad_ref, zblocks.at[zh], device(zh=turn(zh, 1)))
    z_down = send(grad_ref, zblocks.at[zh], device(zh=turn(zh, 3)))
    crossed = [cross(0, grad_ref)]
    w0 = send_weight(0)
    w1 = send_weight(1)

    turn_weight(2)
    locals_[1].wait()
    locals_[2].wait()
    for part in range(7):
        cols = slice(part * 128, part * 128 + 128)
        gate_value = gate_in[:, cols].astype(jnp.float32)
        up_value = up_in[:, cols].astype(jnp.float32)
        sigmoid_gate = jax.nn.sigmoid(gate_value)
        silu_gate = gate_value * sigmoid_gate
        gate_factor[:, cols] = up_value * sigmoid_gate * (1.0 + gate_value * (1.0 - sigmoid_gate))
        up_factor[:, cols] = silu_gate
        hidden[:, cols] = (silu_gate * up_value).astype(jnp.bfloat16)

    z_up.wait_recv()
    block = zblocks.at[turn(zh, 3), pl.ds(0, 32)]
    z_on_up = send(block, block, device(zh=turn(zh, 1)))
    crossed.append(cross(3, zblocks.at[turn(zh, 3)]))
    z_down.wait_recv()
    block = zblocks.at[turn(zh, 1), pl.ds(32, 32)]
    z_on_down = send(block, block, device(zh=turn(zh, 3)))
    crossed.append(cross(1, zblocks.at[turn(zh, 1)]))

    w0_on = forward_weight(0, w0)
    w1_on = forward_weight(1, w1)
    w2 = send_weight(2)
    turn_weight(3, 4)
    for part in range(4):
        up_proj[part] = projection_t(up_seed_ref[0], (part * 4 + zl) * WIDTH, WIDTH)

    z_on_up.wait_recv()
    z_on_down.wait_recv()
    crossed.append(cross(2, zblocks.at[turn(zh, 2)]))
    w3 = send_weight(3)
    w2_on = forward_weight(2, w2)
    turn_weight(5, 6)
    down_proj[...] = projection_t(down_seed_ref[0], col * HID, HID)
    hidden_ranks = lax.dot_general(
        down_proj[...], hidden[...], NT, preferred_element_type=jnp.float32
    ) * (1.0 / math.sqrt(FF * 5461.25))

    pltpu.make_async_copy(grad_ref, grads.at[x, mine(y)], local_sem.at[3]).wait()
    for step in (1, 2, 3):
        source = turn(x, step)
        slot = grads.at[source, mine(y)]
        pltpu.make_async_remote_copy(
            src_ref=slot, dst_ref=slot, send_sem=cross_send.at[step], recv_sem=cross_recv.at[source],
            device_id=device(x=source), device_id_type=MESH,
        ).wait_recv()

    def y_block(source, first=0, count=4):
        return grads.at[pl.ds(first, count), mine(source)]

    side, inner = lax.div(zl, 2), lax.rem(zl + lax.div(zl, 2), 2) == 1
    mate = side * 2 + 1 - lax.rem(zl, 2)

    def is_across(target):
        return lax.div(target, 2) != side

    def part_copy(chunk, kind, target, source=None):
        if chunk == RANKS:
            at = ()
        else:
            at = (pl.ds(*CHUNKS[chunk]),)
        src = (rank_out if chunk == RANKS else part_out).at[(target,) + at]
        if kind == 1:
            slot = lax.rem(target, 2)
            dst = (rank_on if chunk == RANKS else part_on).at[(slot,) + at]
            sem = 2 + slot
        else:
            slot = 0 if kind == 0 else 1
            if kind == 2 and chunk in DIRECT:
                slot = 1 + lax.rem(zl, 2) if source is None else source
            dst = (rank_in if chunk == RANKS else part_in).at[(slot,) + at]
            sem = slot
        return pltpu.make_async_remote_copy(
            src_ref=src, dst_ref=dst, send_sem=part_send.at[chunk * 4 + target],
            recv_sem=part_recv.at[chunk * 4 + sem],
            device_id=device(zl=target if kind == 2 else mate), device_id_type=MESH,
        )

    def wait_parts(chunk):
        part_copy(chunk, 0, mate).wait_recv()
        part_copy(chunk, 2, lax.rem(zl + 2, 4), 1).wait_recv()
        if chunk in DIRECT:
            part_copy(chunk, 2, lax.rem(zl + 2, 4), 2).wait_recv()

    def put(chunk, target, total):
        if chunk == RANKS:
            rank_out[target] = total.astype(jnp.bfloat16)
        else:
            first, count = CHUNKS[chunk]
            for lane in range(count):
                part_out[target, first + lane] = total[:, lane * 128 : lane * 128 + 128].astype(
                    jnp.bfloat16
                )

    pending = []

    def multiply(chunk, target):
        tokens = pl.ds(pl.multiple_of(target * TOK, TOK), TOK)
        total = None
        for part in range(4):
            left = grads[part, tokens]
            if chunk == RANKS:
                product = lax.dot_general(
                    left, up_proj[part], NT, preferred_element_type=jnp.float32
                )
            else:
                first, count = CHUNKS[chunk]
                right = [weights[part, first + piece] for piece in range(count)]
                right = jnp.concatenate(right, axis=1) if count > 1 else right[0]
                product = jnp.dot(left, right, preferred_element_type=jnp.float32)
            total = product if part == 0 else total + product

        keep = target == zl
        if chunk not in DIRECT:
            keep |= is_across(target) & inner

        @pl.when(keep)
        def _():
            if chunk == RANKS:
                rank_own[target] = total
            else:
                own[target, :, first * 128 : (first + count) * 128] = total

        @pl.when(target == mate)
        def _():
            put(chunk, target, total)
            part_copy(chunk, 0, target).start()

        if chunk in DIRECT:

            @pl.when(is_across(target))
            def _():
                put(chunk, target, total)
                part_copy(chunk, 2, target).start()

        else:

            @pl.when(is_across(target) & jnp.logical_not(inner))
            def _():
                put(chunk, target, total)
                part_copy(chunk, 1, target).start()

            pending.append((chunk, target))

    def relay(most=0):
        while len(pending) > most:
            chunk, target = pending.pop(0)

            @pl.when(is_across(target) & inner)
            def _(chunk=chunk, target=target):
                part_copy(chunk, 1, target).wait_recv()
                slot = lax.rem(target, 2)
                if chunk == RANKS:
                    put(chunk, target, rank_own[target] + rank_on[slot].astype(jnp.float32))
                else:
                    first, count = CHUNKS[chunk]
                    for lane in range(first, first + count):
                        part_out[target, lane] = (
                            own[target, :, lane * 128 : lane * 128 + 128]
                            + part_on[slot, lane].astype(jnp.float32)
                        ).astype(jnp.bfloat16)
                part_copy(chunk, 2, target).start()

    def multiply_all(chunk):
        for target in (2 - side * 2, 3 - side * 2, mate, zl):
            multiply(chunk, target)

    def finish(chunk):
        wait_parts(chunk)
        first, count = CHUNKS[chunk]
        for lane in range(first, first + count):
            cols = slice(lane * 128, lane * 128 + 128)
            total = own[zl, :, cols]
            for source in range(3 if chunk in DIRECT else 2):
                total += part_in[source, lane].astype(jnp.float32)
            gate_out[:, cols] = (total * gate_factor[:, cols]).astype(jnp.bfloat16)
            up_out[:, cols] = (total * up_factor[:, cols]).astype(jnp.bfloat16)

    block = y_block(y)
    across = [send(block, block, sibling)]
    y_up = send(block, block, device(y=turn(y, 1)))
    y_down = send(block, block, device(y=turn(y, 3)))
    w4 = send_weight(4)
    w3_on = forward_weight(3, w3)

    across[0].wait_recv()
    multiply(RANKS, turn(y, 0))
    wait_weights(w0_on, w1_on)
    multiply(0, turn(y, 0))
    w5 = send_weight(5)

    relay()
    y_up.wait_recv()
    block = y_block(turn(y, 3))
    across.append(send(block, block, sibling))
    block = y_block(turn(y, 3), 0, 2)
    y_on_up = send(block, block, device(y=turn(y, 1)))
    y_down.wait_recv()
    block = y_block(turn(y, 1))
    across.append(send(block, block, sibling))
    block = y_block(turn(y, 1), 2, 2)
    y_on_down = send(block, block, device(y=turn(y, 3)))
    wait_weights(w2_on, w3_on)
    multiply(1, turn(y, 0))
    relay()
    w4_on = forward_weight(4, w4)
    w6 = send_weight(6)

    for place, step in ((1, 3), (2, 1)):
        across[place].wait_recv()
        multiply(RANKS, turn(y, step))
        multiply(0, turn(y, step))
        relay(2)
    y_on_up.wait_recv()
    block = y_block(turn(y, 2), 0, 2)
    across.append(send(block, block, sibling))
    y_on_down.wait_recv()
    block = y_block(turn(y, 2), 2, 2)
    across.append(send(block, block, sibling))
    multiply(1, turn(y, 3))
    multiply(1, turn(y, 1))
    relay()
    w5_on = forward_weight(5, w5)

    across[3].wait_recv()
    across[4].wait_recv()
    multiply(RANKS, turn(y, 2))
    multiply(0, turn(y, 2))
    relay(2)
    multiply(1, turn(y, 2))
    wait_weights(w4_on)
    multiply_all(2)
    relay()
    w6_on = forward_weight(6, w6)

    wait_parts(RANKS)
    grad_ranks = rank_own[zl]
    for source in range(2):
        grad_ranks += rank_in[source].astype(jnp.float32)
    grad_ranks *= 1.0 / math.sqrt(D * 5461.25)
    live_count = counts_ref[0]
    positions = lax.broadcasted_iota(jnp.int32, (RANK, TOK), 1)
    masked = hidden_ranks * jnp.where(positions < live_count, 1.0, 0.0)
    features = jnp.dot(
        masked, grad_ranks, precision=lax.Precision.HIGHEST, preferred_element_type=jnp.float32
    )
    feat_y[...] = jnp.zeros_like(feat_y)
    for owner in range(32):
        slot = owner // 2 % 4 * 8 + owner // 8 * 2 + owner % 2
        feat_y[slot, 0:2, 0:RANK] = features[owner * 2 : owner * 2 + 2, :]
    y_copies = [
        send(
            feat_y.at[pl.ds(turn(y, step) * 8, 8)], feat_y_in.at[step - 1],
            device(y=turn(y, step)),
        )
        for step in (1, 2, 3)
    ]

    wait_weights(w5_on)
    multiply_all(3)
    relay()
    for copy in y_copies:
        copy.wait_recv()
    feat_z[...] = feat_y[pl.ds(y * 8, 8)] + feat_y_in[0] + feat_y_in[1] + feat_y_in[2]
    z_copies = [
        send(
            feat_z.at[pl.ds(turn(zh, step) * 2, 2)], feat_z_in.at[step - 1],
            device(zh=turn(zh, step)),
        )
        for step in (1, 2, 3)
    ]
    finish(0)

    wait_weights(w6_on)
    multiply_all(4)
    relay()
    finish(1)
    for copy in z_copies:
        copy.wait_recv()
    feat_c[...] = feat_z[pl.ds(zh * 2, 2)] + feat_z_in[0] + feat_z_in[1] + feat_z_in[2]
    c_copy = send(feat_c.at[1 - c], feat_c_in, sibling)
    finish(2)
    c_copy.wait_recv()
    counted = jnp.full((8, 128), live_count, jnp.int32).astype(jnp.float32)
    result = (feat_c[c] + feat_c_in[...]) * lax.rsqrt(counted)
    feat_out[0] = result[0:2, 0:RANK]
    finish(3)
    finish(4)

    for chunk in range(RANKS + 1):
        for target in range(4):

            @pl.when(zl != target)
            def _(chunk=chunk, target=target):
                part_copy(chunk, 2, target).wait_send()

    for copy in started:
        copy.wait_send()
    for target, remote in crossed:

        @pl.when(target != x)
        def _(remote=remote):
            remote.wait_send()


def shards(grad_out, gate_act, up_act, down_weight, counts, down_seed, up_seed):
    hbm = pl.BlockSpec(memory_space=pltpu.HBM)
    smem = pl.BlockSpec(memory_space=pltpu.SMEM)
    vmem = pl.BlockSpec(memory_space=pltpu.VMEM)
    bf16, f32 = jnp.bfloat16, jnp.float32
    return pl.pallas_call(
        kernel,
        out_shape=(
            pltpu.VMEM((TOK, HID), bf16),
            pltpu.VMEM((TOK, HID), bf16),
            pltpu.VMEM((1, 2, RANK), f32),
        ),
        in_specs=[hbm, hbm, hbm, hbm, smem, smem, smem],
        out_specs=(vmem, vmem, vmem),
        scratch_shapes=[
            pltpu.VMEM((TOK, HID), bf16),
            pltpu.VMEM((TOK, HID), bf16),
            pltpu.VMEM((HID, WIDTH), bf16),
            pltpu.VMEM((4, 7, WIDTH, 128), bf16),
            pltpu.VMEM((4, PIECE, WIDTH), bf16),
            pltpu.VMEM((4, 4 * TOK, WIDTH), bf16),
            pltpu.VMEM((4, RANK, WIDTH), bf16),
            pltpu.VMEM((RANK, HID), bf16),
            pltpu.VMEM((TOK, HID), bf16),
            pltpu.VMEM((TOK, HID), f32),
            pltpu.VMEM((TOK, HID), f32),
            pltpu.VMEM((4, TOK, HID), f32),
            pltpu.VMEM((4, 7, TOK, 128), bf16),
            pltpu.VMEM((2, 7, TOK, 128), bf16),
            pltpu.VMEM((3, 7, TOK, 128), bf16),
            pltpu.VMEM((4, TOK, RANK), f32),
            pltpu.VMEM((4, TOK, RANK), bf16),
            pltpu.VMEM((2, TOK, RANK), bf16),
            pltpu.VMEM((2, TOK, RANK), bf16),
            pltpu.VMEM((32, 8, 128), f32),
            pltpu.VMEM((3, 8, 8, 128), f32),
            pltpu.VMEM((8, 8, 128), f32),
            pltpu.VMEM((3, 2, 8, 128), f32),
            pltpu.VMEM((2, 8, 128), f32),
            pltpu.VMEM((8, 128), f32),
            pltpu.SemaphoreType.DMA((COPIES,)),
            pltpu.SemaphoreType.DMA((COPIES,)),
            pltpu.SemaphoreType.DMA((4,)),
            pltpu.SemaphoreType.DMA((4,)),
            pltpu.SemaphoreType.DMA((4,)),
            pltpu.SemaphoreType.DMA((4 * RANKS + 4,)),
            pltpu.SemaphoreType.DMA((4 * RANKS + 4,)),
        ],
        compiler_params=pltpu.CompilerParams(
            collective_id=0, has_side_effects=True, vmem_limit_bytes=60 * 1024 * 1024
        ),
    )(grad_out, gate_act, up_act, down_weight, counts, down_seed, up_seed)


def solution(mesh):
    in_specs = (
        P("col", "row"),
        P("row", "col"),
        P("row", "col"),
        P("col", "row"),
        P("row"),
        P(),
        P(),
    )
    out_specs = (P("row", "col"), P("row", "col"), P("row", "col", None))
    return jax.shard_map(shards, mesh=mesh, in_specs=in_specs, out_specs=out_specs, check_vma=False)
```

```python
import math

import jax
import jax.numpy as jnp
from jax import lax
from jax.experimental import pallas as pl
from jax.experimental.pallas import tpu as pltpu
from jax.sharding import PartitionSpec as P

D = 8192
FF = 28672
RANK = 64
TOK = 128
PIECE = 64
WIDTH = 512
HID = 896
CHUNKS = ((0, 2), (2, 2), (4, 1), (5, 1), (6, 1))
DIRECT = (4,)
RANKS = len(CHUNKS)
NT = (((1,), (1,)), ((), ()))
MESH = pl.DeviceIdType.MESH
COPIES = 96


def scramble(values):
    values = values ^ values >> 16 & 65535
    values = values * 73244475
    values = values ^ values >> 16 & 65535
    values = values * 73244475
    return values ^ values >> 16 & 65535


def projection_t(seed_value, first_row, row_count):
    row_number = first_row + lax.broadcasted_iota(jnp.int32, (RANK, row_count), 1)
    rank_number = lax.broadcasted_iota(jnp.int32, (RANK, row_count), 0)
    seed_mix = scramble(seed_value + 40503)
    hashed = scramble(row_number * RANK + rank_number ^ seed_mix)
    return ((hashed >> 8 & 255).astype(jnp.float32) - 127.5).astype(jnp.bfloat16)


def kernel(
    grad_ref, gate_ref, up_ref, weight_ref, counts_ref, down_seed_ref, up_seed_ref,
    gate_out, up_out, feat_out,
    gate_in, up_in, weight_in, weights, zblocks, grads, up_proj, down_proj, hidden,
    gate_factor, up_factor, own, part_out, part_on, part_in, rank_own, rank_out, rank_on, rank_in,
    feat_y, feat_y_in, feat_z, feat_z_in, feat_c, feat_c_in,
    send_sem, recv_sem, local_sem, cross_send, cross_recv, part_send, part_recv,
):
    row = lax.axis_index("row")
    col = lax.axis_index("col")
    x, zl = lax.div(row, 4), lax.rem(row, 4)
    zh, y, c = lax.div(col, 8), lax.rem(lax.div(col, 2), 4), lax.rem(col, 2)

    def turn(value, step):
        return lax.rem(value + step, 4)

    def device(x=x, zl=zl, zh=zh, y=y, c=c):
        return (x * 4 + zl, (zh * 4 + y) * 2 + c)

    sibling = device(c=1 - c)
    started = []

    def send(src, dst, target):
        index = len(started)
        copy = pltpu.make_async_remote_copy(
            src_ref=src, dst_ref=dst, send_sem=send_sem.at[index], recv_sem=recv_sem.at[index],
            device_id=target, device_id_type=MESH,
        )
        copy.start()
        started.append(copy)
        return copy

    locals_ = []
    for number, (src, dst) in enumerate(
        ((weight_ref, weight_in), (gate_ref, gate_in), (up_ref, up_in))
    ):
        copy = pltpu.make_async_copy(src, dst, local_sem.at[number])
        copy.start()
        locals_.append(copy)

    barrier = pltpu.get_barrier_semaphore()
    peers = [sibling]
    for step in (1, 2, 3):
        peers += [
            device(x=turn(x, step)), device(zl=turn(zl, step)),
            device(zh=turn(zh, step)), device(y=turn(y, step)),
        ]
    for peer in peers:
        pl.semaphore_signal(barrier, inc=1, device_id=peer, device_id_type=MESH)

    locals_[0].wait()
    def turn_weight(*pieces):
        for piece in pieces:
            weights[x, piece] = weight_in[piece * 128 : piece * 128 + 128, :].T

    turn_weight(0, 1)
    pl.semaphore_wait(barrier, len(peers))


    def mine(group):
        return pl.ds(pl.multiple_of(group * TOK + c * PIECE, PIECE), PIECE)

    def cross(step, src):
        target = turn(zh, step)
        slot = grads.at[x, mine(y)]
        remote = pltpu.make_async_remote_copy(
            src_ref=src, dst_ref=slot, send_sem=cross_send.at[step], recv_sem=cross_recv.at[x],
            device_id=device(x=target), device_id_type=MESH,
        )
        local = pltpu.make_async_copy(src, slot, local_sem.at[3])

        @pl.when(target != x)
        def _():
            remote.start()

        @pl.when(target == x)
        def _():
            local.start()

        return target, remote

    def send_weight(piece):
        block = weights.at[x, piece]
        right = send(block, block, device(x=turn(x, 1)))
        left = send(block, block, device(x=turn(x, 3)))
        return right, left

    def forward_weight(piece, copies):
        right, left = copies
        right.wait_recv()
        block = weights.at[turn(x, 3), piece, pl.ds(0, WIDTH // 2)]
        on_right = send(block, block, device(x=turn(x, 1)))
        left.wait_recv()
        block = weights.at[turn(x, 1), piece, pl.ds(WIDTH // 2, WIDTH // 2)]
        on_left = send(block, block, device(x=turn(x, 3)))
        return on_right, on_left

    def wait_weights(*pieces):
        for copies in pieces:
            for copy in copies:
                copy.wait_recv()

    z_up = send(grad_ref, zblocks.at[zh], device(zh=turn(zh, 1)))
    z_down = send(grad_ref, zblocks.at[zh], device(zh=turn(zh, 3)))
    crossed = [cross(0, grad_ref)]
    w0 = send_weight(0)
    w1 = send_weight(1)

    turn_weight(2)
    locals_[1].wait()
    locals_[2].wait()
    for part in range(7):
        cols = slice(part * 128, part * 128 + 128)
        gate_value = gate_in[:, cols].astype(jnp.float32)
        up_value = up_in[:, cols].astype(jnp.float32)
        sigmoid_gate = jax.nn.sigmoid(gate_value)
        silu_gate = gate_value * sigmoid_gate
        gate_factor[:, cols] = up_value * sigmoid_gate * (1.0 + gate_value * (1.0 - sigmoid_gate))
        up_factor[:, cols] = silu_gate
        hidden[:, cols] = (silu_gate * up_value).astype(jnp.bfloat16)

    z_up.wait_recv()
    block = zblocks.at[turn(zh, 3), pl.ds(0, 32)]
    z_on_up = send(block, block, device(zh=turn(zh, 1)))
    crossed.append(cross(3, zblocks.at[turn(zh, 3)]))
    z_down.wait_recv()
    block = zblocks.at[turn(zh, 1), pl.ds(32, 32)]
    z_on_down = send(block, block, device(zh=turn(zh, 3)))
    crossed.append(cross(1, zblocks.at[turn(zh, 1)]))

    w0_on = forward_weight(0, w0)
    w1_on = forward_weight(1, w1)
    w2 = send_weight(2)
    turn_weight(3, 4)
    for part in range(4):
        up_proj[part] = projection_t(up_seed_ref[0], (part * 4 + zl) * WIDTH, WIDTH)

    z_on_up.wait_recv()
    z_on_down.wait_recv()
    crossed.append(cross(2, zblocks.at[turn(zh, 2)]))
    w3 = send_weight(3)
    w2_on = forward_weight(2, w2)
    turn_weight(5, 6)
    down_proj[...] = projection_t(down_seed_ref[0], col * HID, HID)
    hidden_ranks = lax.dot_general(
        down_proj[...], hidden[...], NT, preferred_element_type=jnp.float32
    ) * (1.0 / math.sqrt(FF * 5461.25))

    pltpu.make_async_copy(grad_ref, grads.at[x, mine(y)], local_sem.at[3]).wait()
    for step in (1, 2, 3):
        source = turn(x, step)
        slot = grads.at[source, mine(y)]
        pltpu.make_async_remote_copy(
            src_ref=slot, dst_ref=slot, send_sem=cross_send.at[step], recv_sem=cross_recv.at[source],
            device_id=device(x=source), device_id_type=MESH,
        ).wait_recv()

    def y_block(source, first=0, count=4):
        return grads.at[pl.ds(first, count), mine(source)]

    side, inner = lax.div(zl, 2), lax.rem(zl + lax.div(zl, 2), 2) == 1
    mate = side * 2 + 1 - lax.rem(zl, 2)

    def is_across(target):
        return lax.div(target, 2) != side

    def part_copy(chunk, kind, target, source=None):
        if chunk == RANKS:
            at = ()
        else:
            at = (pl.ds(*CHUNKS[chunk]),)
        src = (rank_out if chunk == RANKS else part_out).at[(target,) + at]
        if kind == 1:
            slot = lax.rem(target, 2)
            dst = (rank_on if chunk == RANKS else part_on).at[(slot,) + at]
            sem = 2 + slot
        else:
            slot = 0 if kind == 0 else 1
            if kind == 2 and chunk in DIRECT:
                slot = 1 + lax.rem(zl, 2) if source is None else source
            dst = (rank_in if chunk == RANKS else part_in).at[(slot,) + at]
            sem = slot
        return pltpu.make_async_remote_copy(
            src_ref=src, dst_ref=dst, send_sem=part_send.at[chunk * 4 + target],
            recv_sem=part_recv.at[chunk * 4 + sem],
            device_id=device(zl=target if kind == 2 else mate), device_id_type=MESH,
        )

    def wait_parts(chunk):
        part_copy(chunk, 0, mate).wait_recv()
        part_copy(chunk, 2, lax.rem(zl + 2, 4), 1).wait_recv()
        if chunk in DIRECT:
            part_copy(chunk, 2, lax.rem(zl + 2, 4), 2).wait_recv()

    def put(chunk, target, total):
        if chunk == RANKS:
            rank_out[target] = total.astype(jnp.bfloat16)
        else:
            first, count = CHUNKS[chunk]
            for lane in range(count):
                part_out[target, first + lane] = total[:, lane * 128 : lane * 128 + 128].astype(
                    jnp.bfloat16
                )

    pending = []

    def multiply(chunk, target):
        tokens = pl.ds(pl.multiple_of(target * TOK, TOK), TOK)
        total = None
        for part in range(4):
            left = grads[part, tokens]
            if chunk == RANKS:
                product = lax.dot_general(
                    left, up_proj[part], NT, preferred_element_type=jnp.float32
                )
            else:
                first, count = CHUNKS[chunk]
                right = [weights[part, first + piece] for piece in range(count)]
                right = jnp.concatenate(right, axis=1) if count > 1 else right[0]
                product = jnp.dot(left, right, preferred_element_type=jnp.float32)
            total = product if part == 0 else total + product

        keep = target == zl
        if chunk not in DIRECT:
            keep |= is_across(target) & inner

        @pl.when(keep)
        def _():
            if chunk == RANKS:
                rank_own[target] = total
            else:
                own[target, :, first * 128 : (first + count) * 128] = total

        @pl.when(target == mate)
        def _():
            put(chunk, target, total)
            part_copy(chunk, 0, target).start()

        if chunk in DIRECT:

            @pl.when(is_across(target))
            def _():
                put(chunk, target, total)
                part_copy(chunk, 2, target).start()

        else:

            @pl.when(is_across(target) & jnp.logical_not(inner))
            def _():
                put(chunk, target, total)
                part_copy(chunk, 1, target).start()

            pending.append((chunk, target))

    def relay(most=0):
        while len(pending) > most:
            chunk, target = pending.pop(0)

            @pl.when(is_across(target) & inner)
            def _(chunk=chunk, target=target):
                part_copy(chunk, 1, target).wait_recv()
                slot = lax.rem(target, 2)
                if chunk == RANKS:
                    put(chunk, target, rank_own[target] + rank_on[slot].astype(jnp.float32))
                else:
                    first, count = CHUNKS[chunk]
                    for lane in range(first, first + count):
                        part_out[target, lane] = (
                            own[target, :, lane * 128 : lane * 128 + 128]
                            + part_on[slot, lane].astype(jnp.float32)
                        ).astype(jnp.bfloat16)
                part_copy(chunk, 2, target).start()

    def multiply_all(chunk):
        for target in (2 - side * 2, 3 - side * 2, mate, zl):
            multiply(chunk, target)

    def finish(chunk):
        wait_parts(chunk)
        first, count = CHUNKS[chunk]
        for lane in range(first, first + count):
            cols = slice(lane * 128, lane * 128 + 128)
            total = own[zl, :, cols]
            for source in range(3 if chunk in DIRECT else 2):
                total += part_in[source, lane].astype(jnp.float32)
            gate_out[:, cols] = (total * gate_factor[:, cols]).astype(jnp.bfloat16)
            up_out[:, cols] = (total * up_factor[:, cols]).astype(jnp.bfloat16)

    block = y_block(y)
    y_up = send(block, block, device(y=turn(y, 1)))
    y_down = send(block, block, device(y=turn(y, 3)))
    across = [send(block, block, sibling)]
    w4 = send_weight(4)
    w3_on = forward_weight(3, w3)

    across[0].wait_recv()
    multiply(RANKS, turn(y, 0))
    wait_weights(w0_on, w1_on)
    multiply(0, turn(y, 0))
    w5 = send_weight(5)

    relay()
    y_up.wait_recv()
    block = y_block(turn(y, 3), 0, 2)
    y_on_up = send(block, block, device(y=turn(y, 1)))
    block = y_block(turn(y, 3))
    across.append(send(block, block, sibling))
    y_down.wait_recv()
    block = y_block(turn(y, 1), 2, 2)
    y_on_down = send(block, block, device(y=turn(y, 3)))
    block = y_block(turn(y, 1))
    across.append(send(block, block, sibling))
    wait_weights(w2_on, w3_on)
    multiply(1, turn(y, 0))
    relay()
    w4_on = forward_weight(4, w4)
    w6 = send_weight(6)

    for place, step in ((1, 3), (2, 1)):
        across[place].wait_recv()
        multiply(RANKS, turn(y, step))
        multiply(0, turn(y, step))
        relay(2)
    y_on_up.wait_recv()
    block = y_block(turn(y, 2), 0, 2)
    across.append(send(block, block, sibling))
    y_on_down.wait_recv()
    block = y_block(turn(y, 2), 2, 2)
    across.append(send(block, block, sibling))
    multiply(1, turn(y, 3))
    multiply(1, turn(y, 1))
    relay()
    w5_on = forward_weight(5, w5)

    across[3].wait_recv()
    across[4].wait_recv()
    multiply(RANKS, turn(y, 2))
    multiply(0, turn(y, 2))
    relay(2)
    multiply(1, turn(y, 2))
    wait_weights(w4_on)
    multiply_all(2)
    relay()
    w6_on = forward_weight(6, w6)

    wait_parts(RANKS)
    grad_ranks = rank_own[zl]
    for source in range(2):
        grad_ranks += rank_in[source].astype(jnp.float32)
    grad_ranks *= 1.0 / math.sqrt(D * 5461.25)
    live_count = counts_ref[0]
    positions = lax.broadcasted_iota(jnp.int32, (RANK, TOK), 1)
    masked = hidden_ranks * jnp.where(positions < live_count, 1.0, 0.0)
    features = jnp.dot(
        masked, grad_ranks, precision=lax.Precision.HIGHEST, preferred_element_type=jnp.float32
    )
    feat_y[...] = jnp.zeros_like(feat_y)
    for owner in range(32):
        slot = owner // 2 % 4 * 8 + owner // 8 * 2 + owner % 2
        feat_y[slot, 0:2, 0:RANK] = features[owner * 2 : owner * 2 + 2, :]
    y_copies = [
        send(
            feat_y.at[pl.ds(turn(y, step) * 8, 8)], feat_y_in.at[step - 1],
            device(y=turn(y, step)),
        )
        for step in (1, 2, 3)
    ]

    wait_weights(w5_on)
    multiply_all(3)
    relay()
    for copy in y_copies:
        copy.wait_recv()
    feat_z[...] = feat_y[pl.ds(y * 8, 8)] + feat_y_in[0] + feat_y_in[1] + feat_y_in[2]
    z_copies = [
        send(
            feat_z.at[pl.ds(turn(zh, step) * 2, 2)], feat_z_in.at[step - 1],
            device(zh=turn(zh, step)),
        )
        for step in (1, 2, 3)
    ]
    finish(0)

    wait_weights(w6_on)
    multiply_all(4)
    relay()
    finish(1)
    for copy in z_copies:
        copy.wait_recv()
    feat_c[...] = feat_z[pl.ds(zh * 2, 2)] + feat_z_in[0] + feat_z_in[1] + feat_z_in[2]
    c_copy = send(feat_c.at[1 - c], feat_c_in, sibling)
    finish(2)
    c_copy.wait_recv()
    counted = jnp.full((8, 128), live_count, jnp.int32).astype(jnp.float32)
    result = (feat_c[c] + feat_c_in[...]) * lax.rsqrt(counted)
    feat_out[0] = result[0:2, 0:RANK]
    finish(3)
    finish(4)

    for chunk in range(RANKS + 1):
        for target in range(4):

            @pl.when(zl != target)
            def _(chunk=chunk, target=target):
                part_copy(chunk, 2, target).wait_send()

    for copy in started:
        copy.wait_send()
    for target, remote in crossed:

        @pl.when(target != x)
        def _(remote=remote):
            remote.wait_send()


def shards(grad_out, gate_act, up_act, down_weight, counts, down_seed, up_seed):
    hbm = pl.BlockSpec(memory_space=pltpu.HBM)
    smem = pl.BlockSpec(memory_space=pltpu.SMEM)
    vmem = pl.BlockSpec(memory_space=pltpu.VMEM)
    bf16, f32 = jnp.bfloat16, jnp.float32
    return pl.pallas_call(
        kernel,
        out_shape=(
            pltpu.VMEM((TOK, HID), bf16),
            pltpu.VMEM((TOK, HID), bf16),
            pltpu.VMEM((1, 2, RANK), f32),
        ),
        in_specs=[hbm, hbm, hbm, hbm, smem, smem, smem],
        out_specs=(vmem, vmem, vmem),
        scratch_shapes=[
            pltpu.VMEM((TOK, HID), bf16),
            pltpu.VMEM((TOK, HID), bf16),
            pltpu.VMEM((HID, WIDTH), bf16),
            pltpu.VMEM((4, 7, WIDTH, 128), bf16),
            pltpu.VMEM((4, PIECE, WIDTH), bf16),
            pltpu.VMEM((4, 4 * TOK, WIDTH), bf16),
            pltpu.VMEM((4, RANK, WIDTH), bf16),
            pltpu.VMEM((RANK, HID), bf16),
            pltpu.VMEM((TOK, HID), bf16),
            pltpu.VMEM((TOK, HID), f32),
            pltpu.VMEM((TOK, HID), f32),
            pltpu.VMEM((4, TOK, HID), f32),
            pltpu.VMEM((4, 7, TOK, 128), bf16),
            pltpu.VMEM((2, 7, TOK, 128), bf16),
            pltpu.VMEM((3, 7, TOK, 128), bf16),
            pltpu.VMEM((4, TOK, RANK), f32),
            pltpu.VMEM((4, TOK, RANK), bf16),
            pltpu.VMEM((2, TOK, RANK), bf16),
            pltpu.VMEM((2, TOK, RANK), bf16),
            pltpu.VMEM((32, 8, 128), f32),
            pltpu.VMEM((3, 8, 8, 128), f32),
            pltpu.VMEM((8, 8, 128), f32),
            pltpu.VMEM((3, 2, 8, 128), f32),
            pltpu.VMEM((2, 8, 128), f32),
            pltpu.VMEM((8, 128), f32),
            pltpu.SemaphoreType.DMA((COPIES,)),
            pltpu.SemaphoreType.DMA((COPIES,)),
            pltpu.SemaphoreType.DMA((4,)),
            pltpu.SemaphoreType.DMA((4,)),
            pltpu.SemaphoreType.DMA((4,)),
            pltpu.SemaphoreType.DMA((4 * RANKS + 4,)),
            pltpu.SemaphoreType.DMA((4 * RANKS + 4,)),
        ],
        compiler_params=pltpu.CompilerParams(
            collective_id=0, has_side_effects=True, vmem_limit_bytes=60 * 1024 * 1024
        ),
    )(grad_out, gate_act, up_act, down_weight, counts, down_seed, up_seed)


def solution(mesh):
    in_specs = (
        P("col", "row"),
        P("row", "col"),
        P("row", "col"),
        P("col", "row"),
        P("row"),
        P(),
        P(),
    )
    out_specs = (P("row", "col"), P("row", "col"), P("row", "col", None))
    return jax.shard_map(shards, mesh=mesh, in_specs=in_specs, out_specs=out_specs, check_vma=False)
```

```python
import math

import jax
import jax.numpy as jnp
from jax import lax
from jax.experimental import pallas as pl
from jax.experimental.pallas import tpu as pltpu
from jax.sharding import PartitionSpec as P

D = 8192
FF = 28672
RANK = 64
TOK = 128
PIECE = 64
WIDTH = 512
HID = 896
CHUNKS = ((0, 2), (2, 2), (4, 1), (5, 1), (6, 1))
DIRECT = (3, 4)
RANKS = len(CHUNKS)
NT = (((1,), (1,)), ((), ()))
MESH = pl.DeviceIdType.MESH
COPIES = 96


def scramble(values):
    values = values ^ values >> 16 & 65535
    values = values * 73244475
    values = values ^ values >> 16 & 65535
    values = values * 73244475
    return values ^ values >> 16 & 65535


def projection_t(seed_value, first_row, row_count):
    row_number = first_row + lax.broadcasted_iota(jnp.int32, (RANK, row_count), 1)
    rank_number = lax.broadcasted_iota(jnp.int32, (RANK, row_count), 0)
    seed_mix = scramble(seed_value + 40503)
    hashed = scramble(row_number * RANK + rank_number ^ seed_mix)
    return ((hashed >> 8 & 255).astype(jnp.float32) - 127.5).astype(jnp.bfloat16)


def kernel(
    grad_ref, gate_ref, up_ref, weight_ref, counts_ref, down_seed_ref, up_seed_ref,
    gate_out, up_out, feat_out,
    gate_in, up_in, weight_in, weights, zblocks, grads, up_proj, down_proj, hidden,
    gate_factor, up_factor, own, part_out, part_on, part_in, rank_own, rank_out, rank_on, rank_in,
    feat_y, feat_y_in, feat_z, feat_z_in, feat_c, feat_c_in,
    send_sem, recv_sem, local_sem, cross_send, cross_recv, part_send, part_recv,
):
    row = lax.axis_index("row")
    col = lax.axis_index("col")
    x, zl = lax.div(row, 4), lax.rem(row, 4)
    zh, y, c = lax.div(col, 8), lax.rem(lax.div(col, 2), 4), lax.rem(col, 2)

    def turn(value, step):
        return lax.rem(value + step, 4)

    def device(x=x, zl=zl, zh=zh, y=y, c=c):
        return (x * 4 + zl, (zh * 4 + y) * 2 + c)

    sibling = device(c=1 - c)
    started = []

    def send(src, dst, target):
        index = len(started)
        copy = pltpu.make_async_remote_copy(
            src_ref=src, dst_ref=dst, send_sem=send_sem.at[index], recv_sem=recv_sem.at[index],
            device_id=target, device_id_type=MESH,
        )
        copy.start()
        started.append(copy)
        return copy

    locals_ = []
    for number, (src, dst) in enumerate(
        ((weight_ref, weight_in), (gate_ref, gate_in), (up_ref, up_in))
    ):
        copy = pltpu.make_async_copy(src, dst, local_sem.at[number])
        copy.start()
        locals_.append(copy)

    barrier = pltpu.get_barrier_semaphore()
    peers = [sibling]
    for step in (1, 2, 3):
        peers += [
            device(x=turn(x, step)), device(zl=turn(zl, step)),
            device(zh=turn(zh, step)), device(y=turn(y, step)),
        ]
    for peer in peers:
        pl.semaphore_signal(barrier, inc=1, device_id=peer, device_id_type=MESH)

    def turn_weight(*pieces):
        for piece in pieces:
            weights[x, piece] = weight_in[piece * 128 : piece * 128 + 128, :].T

    pl.semaphore_wait(barrier, len(peers))


    def mine(group):
        return pl.ds(pl.multiple_of(group * TOK + c * PIECE, PIECE), PIECE)

    def cross(step, src):
        target = turn(zh, step)
        slot = grads.at[x, mine(y)]
        remote = pltpu.make_async_remote_copy(
            src_ref=src, dst_ref=slot, send_sem=cross_send.at[step], recv_sem=cross_recv.at[x],
            device_id=device(x=target), device_id_type=MESH,
        )
        local = pltpu.make_async_copy(src, slot, local_sem.at[3])

        @pl.when(target != x)
        def _():
            remote.start()

        @pl.when(target == x)
        def _():
            local.start()

        return target, remote

    def send_weight(piece):
        block = weights.at[x, piece]
        right = send(block, block, device(x=turn(x, 1)))
        left = send(block, block, device(x=turn(x, 3)))
        return right, left

    def forward_weight(piece, copies):
        right, left = copies
        right.wait_recv()
        block = weights.at[turn(x, 3), piece, pl.ds(0, WIDTH // 2)]
        on_right = send(block, block, device(x=turn(x, 1)))
        left.wait_recv()
        block = weights.at[turn(x, 1), piece, pl.ds(WIDTH // 2, WIDTH // 2)]
        on_left = send(block, block, device(x=turn(x, 3)))
        return on_right, on_left

    def wait_weights(*pieces):
        for copies in pieces:
            for copy in copies:
                copy.wait_recv()

    z_up = send(grad_ref, zblocks.at[zh], device(zh=turn(zh, 1)))
    z_down = send(grad_ref, zblocks.at[zh], device(zh=turn(zh, 3)))
    crossed = [cross(0, grad_ref)]
    locals_[0].wait()
    turn_weight(0)
    w0 = send_weight(0)
    turn_weight(1)
    w1 = send_weight(1)

    turn_weight(2)
    locals_[1].wait()
    locals_[2].wait()
    for part in range(7):
        cols = slice(part * 128, part * 128 + 128)
        gate_value = gate_in[:, cols].astype(jnp.float32)
        up_value = up_in[:, cols].astype(jnp.float32)
        sigmoid_gate = jax.nn.sigmoid(gate_value)
        silu_gate = gate_value * sigmoid_gate
        gate_factor[:, cols] = up_value * sigmoid_gate * (1.0 + gate_value * (1.0 - sigmoid_gate))
        up_factor[:, cols] = silu_gate
        hidden[:, cols] = (silu_gate * up_value).astype(jnp.bfloat16)

    z_up.wait_recv()
    block = zblocks.at[turn(zh, 3), pl.ds(0, 32)]
    z_on_up = send(block, block, device(zh=turn(zh, 1)))
    crossed.append(cross(3, zblocks.at[turn(zh, 3)]))
    z_down.wait_recv()
    block = zblocks.at[turn(zh, 1), pl.ds(32, 32)]
    z_on_down = send(block, block, device(zh=turn(zh, 3)))
    crossed.append(cross(1, zblocks.at[turn(zh, 1)]))

    w0_on = forward_weight(0, w0)
    w1_on = forward_weight(1, w1)
    w2 = send_weight(2)
    turn_weight(3, 4)
    for part in range(4):
        up_proj[part] = projection_t(up_seed_ref[0], (part * 4 + zl) * WIDTH, WIDTH)

    z_on_up.wait_recv()
    z_on_down.wait_recv()
    crossed.append(cross(2, zblocks.at[turn(zh, 2)]))
    w3 = send_weight(3)
    w2_on = forward_weight(2, w2)
    turn_weight(5, 6)
    down_proj[...] = projection_t(down_seed_ref[0], col * HID, HID)
    hidden_ranks = lax.dot_general(
        down_proj[...], hidden[...], NT, preferred_element_type=jnp.float32
    ) * (1.0 / math.sqrt(FF * 5461.25))

    pltpu.make_async_copy(grad_ref, grads.at[x, mine(y)], local_sem.at[3]).wait()
    for step in (1, 2, 3):
        source = turn(x, step)
        slot = grads.at[source, mine(y)]
        pltpu.make_async_remote_copy(
            src_ref=slot, dst_ref=slot, send_sem=cross_send.at[step], recv_sem=cross_recv.at[source],
            device_id=device(x=source), device_id_type=MESH,
        ).wait_recv()

    def y_block(source, first=0, count=4):
        return grads.at[pl.ds(first, count), mine(source)]

    side, inner = lax.div(zl, 2), lax.rem(zl + lax.div(zl, 2), 2) == 1
    mate = side * 2 + 1 - lax.rem(zl, 2)

    def is_across(target):
        return lax.div(target, 2) != side

    def part_copy(chunk, kind, target, source=None):
        if chunk == RANKS:
            at = ()
        else:
            at = (pl.ds(*CHUNKS[chunk]),)
        src = (rank_out if chunk == RANKS else part_out).at[(target,) + at]
        if kind == 1:
            slot = lax.rem(target, 2)
            dst = (rank_on if chunk == RANKS else part_on).at[(slot,) + at]
            sem = 2 + slot
        else:
            slot = 0 if kind == 0 else 1
            if kind == 2 and chunk in DIRECT:
                slot = 1 + lax.rem(zl, 2) if source is None else source
            dst = (rank_in if chunk == RANKS else part_in).at[(slot,) + at]
            sem = slot
        return pltpu.make_async_remote_copy(
            src_ref=src, dst_ref=dst, send_sem=part_send.at[chunk * 4 + target],
            recv_sem=part_recv.at[chunk * 4 + sem],
            device_id=device(zl=target if kind == 2 else mate), device_id_type=MESH,
        )

    def wait_parts(chunk):
        part_copy(chunk, 0, mate).wait_recv()
        part_copy(chunk, 2, lax.rem(zl + 2, 4), 1).wait_recv()
        if chunk in DIRECT:
            part_copy(chunk, 2, lax.rem(zl + 2, 4), 2).wait_recv()

    def put(chunk, target, total):
        if chunk == RANKS:
            rank_out[target] = total.astype(jnp.bfloat16)
        else:
            first, count = CHUNKS[chunk]
            for lane in range(count):
                part_out[target, first + lane] = total[:, lane * 128 : lane * 128 + 128].astype(
                    jnp.bfloat16
                )

    pending = []

    def multiply(chunk, target):
        tokens = pl.ds(pl.multiple_of(target * TOK, TOK), TOK)
        total = None
        for part in range(4):
            left = grads[part, tokens]
            if chunk == RANKS:
                product = lax.dot_general(
                    left, up_proj[part], NT, preferred_element_type=jnp.float32
                )
            else:
                first, count = CHUNKS[chunk]
                right = [weights[part, first + piece] for piece in range(count)]
                right = jnp.concatenate(right, axis=1) if count > 1 else right[0]
                product = jnp.dot(left, right, preferred_element_type=jnp.float32)
            total = product if part == 0 else total + product

        keep = target == zl
        if chunk not in DIRECT:
            keep |= is_across(target) & inner

        @pl.when(keep)
        def _():
            if chunk == RANKS:
                rank_own[target] = total
            else:
                own[target, :, first * 128 : (first + count) * 128] = total

        @pl.when(target == mate)
        def _():
            put(chunk, target, total)
            part_copy(chunk, 0, target).start()

        if chunk in DIRECT:

            @pl.when(is_across(target))
            def _():
                put(chunk, target, total)
                part_copy(chunk, 2, target).start()

        else:

            @pl.when(is_across(target) & jnp.logical_not(inner))
            def _():
                put(chunk, target, total)
                part_copy(chunk, 1, target).start()

            pending.append((chunk, target))

    def relay(most=0):
        while len(pending) > most:
            chunk, target = pending.pop(0)

            @pl.when(is_across(target) & inner)
            def _(chunk=chunk, target=target):
                part_copy(chunk, 1, target).wait_recv()
                slot = lax.rem(target, 2)
                if chunk == RANKS:
                    put(chunk, target, rank_own[target] + rank_on[slot].astype(jnp.float32))
                else:
                    first, count = CHUNKS[chunk]
                    for lane in range(first, first + count):
                        part_out[target, lane] = (
                            own[target, :, lane * 128 : lane * 128 + 128]
                            + part_on[slot, lane].astype(jnp.float32)
                        ).astype(jnp.bfloat16)
                part_copy(chunk, 2, target).start()

    def multiply_all(chunk):
        for target in (2 - side * 2, 3 - side * 2, mate, zl):
            multiply(chunk, target)

    def finish(chunk):
        wait_parts(chunk)
        first, count = CHUNKS[chunk]
        for lane in range(first, first + count):
            cols = slice(lane * 128, lane * 128 + 128)
            total = own[zl, :, cols]
            for source in range(3 if chunk in DIRECT else 2):
                total += part_in[source, lane].astype(jnp.float32)
            gate_out[:, cols] = (total * gate_factor[:, cols]).astype(jnp.bfloat16)
            up_out[:, cols] = (total * up_factor[:, cols]).astype(jnp.bfloat16)

    block = y_block(y)
    y_up = send(block, block, device(y=turn(y, 1)))
    y_down = send(block, block, device(y=turn(y, 3)))
    across = [send(block, block, sibling)]
    w4 = send_weight(4)
    w3_on = forward_weight(3, w3)

    across[0].wait_recv()
    multiply(RANKS, turn(y, 0))
    wait_weights(w0_on, w1_on)
    multiply(0, turn(y, 0))
    w5 = send_weight(5)

    relay()
    y_up.wait_recv()
    block = y_block(turn(y, 3), 0, 2)
    y_on_up = send(block, block, device(y=turn(y, 1)))
    block = y_block(turn(y, 3))
    across.append(send(block, block, sibling))
    y_down.wait_recv()
    block = y_block(turn(y, 1), 2, 2)
    y_on_down = send(block, block, device(y=turn(y, 3)))
    block = y_block(turn(y, 1))
    across.append(send(block, block, sibling))
    wait_weights(w2_on, w3_on)
    multiply(1, turn(y, 0))
    relay()
    w4_on = forward_weight(4, w4)
    w6 = send_weight(6)

    for place, step in ((1, 3), (2, 1)):
        across[place].wait_recv()
        multiply(RANKS, turn(y, step))
        multiply(0, turn(y, step))
        relay(2)
    y_on_up.wait_recv()
    block = y_block(turn(y, 2), 0, 2)
    across.append(send(block, block, sibling))
    y_on_down.wait_recv()
    block = y_block(turn(y, 2), 2, 2)
    across.append(send(block, block, sibling))
    multiply(1, turn(y, 3))
    multiply(1, turn(y, 1))
    relay()
    w5_on = forward_weight(5, w5)

    across[3].wait_recv()
    across[4].wait_recv()
    multiply(RANKS, turn(y, 2))
    multiply(0, turn(y, 2))
    relay(2)
    multiply(1, turn(y, 2))
    wait_weights(w4_on)
    multiply_all(2)
    relay()
    w6_on = forward_weight(6, w6)

    wait_parts(RANKS)
    grad_ranks = rank_own[zl]
    for source in range(2):
        grad_ranks += rank_in[source].astype(jnp.float32)
    grad_ranks *= 1.0 / math.sqrt(D * 5461.25)
    live_count = counts_ref[0]
    positions = lax.broadcasted_iota(jnp.int32, (RANK, TOK), 1)
    masked = hidden_ranks * jnp.where(positions < live_count, 1.0, 0.0)
    features = jnp.dot(
        masked, grad_ranks, precision=lax.Precision.HIGHEST, preferred_element_type=jnp.float32
    )
    feat_y[...] = jnp.zeros_like(feat_y)
    for owner in range(32):
        slot = owner // 2 % 4 * 8 + owner // 8 * 2 + owner % 2
        feat_y[slot, 0:2, 0:RANK] = features[owner * 2 : owner * 2 + 2, :]
    y_copies = [
        send(
            feat_y.at[pl.ds(turn(y, step) * 8, 8)], feat_y_in.at[step - 1],
            device(y=turn(y, step)),
        )
        for step in (1, 2, 3)
    ]

    wait_weights(w5_on)
    multiply_all(3)
    relay()
    for copy in y_copies:
        copy.wait_recv()
    feat_z[...] = feat_y[pl.ds(y * 8, 8)] + feat_y_in[0] + feat_y_in[1] + feat_y_in[2]
    z_copies = [
        send(
            feat_z.at[pl.ds(turn(zh, step) * 2, 2)], feat_z_in.at[step - 1],
            device(zh=turn(zh, step)),
        )
        for step in (1, 2, 3)
    ]
    finish(0)

    wait_weights(w6_on)
    multiply_all(4)
    relay()
    finish(1)
    for copy in z_copies:
        copy.wait_recv()
    feat_c[...] = feat_z[pl.ds(zh * 2, 2)] + feat_z_in[0] + feat_z_in[1] + feat_z_in[2]
    c_copy = send(feat_c.at[1 - c], feat_c_in, sibling)
    finish(2)
    c_copy.wait_recv()
    counted = jnp.full((8, 128), live_count, jnp.int32).astype(jnp.float32)
    result = (feat_c[c] + feat_c_in[...]) * lax.rsqrt(counted)
    feat_out[0] = result[0:2, 0:RANK]
    finish(3)
    finish(4)

    for chunk in range(RANKS + 1):
        for target in range(4):

            @pl.when(zl != target)
            def _(chunk=chunk, target=target):
                part_copy(chunk, 2, target).wait_send()

    for copy in started:
        copy.wait_send()
    for target, remote in crossed:

        @pl.when(target != x)
        def _(remote=remote):
            remote.wait_send()


def shards(grad_out, gate_act, up_act, down_weight, counts, down_seed, up_seed):
    hbm = pl.BlockSpec(memory_space=pltpu.HBM)
    smem = pl.BlockSpec(memory_space=pltpu.SMEM)
    vmem = pl.BlockSpec(memory_space=pltpu.VMEM)
    bf16, f32 = jnp.bfloat16, jnp.float32
    return pl.pallas_call(
        kernel,
        out_shape=(
            pltpu.VMEM((TOK, HID), bf16),
            pltpu.VMEM((TOK, HID), bf16),
            pltpu.VMEM((1, 2, RANK), f32),
        ),
        in_specs=[hbm, hbm, hbm, hbm, smem, smem, smem],
        out_specs=(vmem, vmem, vmem),
        scratch_shapes=[
            pltpu.VMEM((TOK, HID), bf16),
            pltpu.VMEM((TOK, HID), bf16),
            pltpu.VMEM((HID, WIDTH), bf16),
            pltpu.VMEM((4, 7, WIDTH, 128), bf16),
            pltpu.VMEM((4, PIECE, WIDTH), bf16),
            pltpu.VMEM((4, 4 * TOK, WIDTH), bf16),
            pltpu.VMEM((4, RANK, WIDTH), bf16),
            pltpu.VMEM((RANK, HID), bf16),
            pltpu.VMEM((TOK, HID), bf16),
            pltpu.VMEM((TOK, HID), f32),
            pltpu.VMEM((TOK, HID), f32),
            pltpu.VMEM((4, TOK, HID), f32),
            pltpu.VMEM((4, 7, TOK, 128), bf16),
            pltpu.VMEM((2, 7, TOK, 128), bf16),
            pltpu.VMEM((3, 7, TOK, 128), bf16),
            pltpu.VMEM((4, TOK, RANK), f32),
            pltpu.VMEM((4, TOK, RANK), bf16),
            pltpu.VMEM((2, TOK, RANK), bf16),
            pltpu.VMEM((2, TOK, RANK), bf16),
            pltpu.VMEM((32, 8, 128), f32),
            pltpu.VMEM((3, 8, 8, 128), f32),
            pltpu.VMEM((8, 8, 128), f32),
            pltpu.VMEM((3, 2, 8, 128), f32),
            pltpu.VMEM((2, 8, 128), f32),
            pltpu.VMEM((8, 128), f32),
            pltpu.SemaphoreType.DMA((COPIES,)),
            pltpu.SemaphoreType.DMA((COPIES,)),
            pltpu.SemaphoreType.DMA((4,)),
            pltpu.SemaphoreType.DMA((4,)),
            pltpu.SemaphoreType.DMA((4,)),
            pltpu.SemaphoreType.DMA((4 * RANKS + 4,)),
            pltpu.SemaphoreType.DMA((4 * RANKS + 4,)),
        ],
        compiler_params=pltpu.CompilerParams(
            collective_id=0, has_side_effects=True, vmem_limit_bytes=60 * 1024 * 1024
        ),
    )(grad_out, gate_act, up_act, down_weight, counts, down_seed, up_seed)


def solution(mesh):
    in_specs = (
        P("col", "row"),
        P("row", "col"),
        P("row", "col"),
        P("col", "row"),
        P("row"),
        P(),
        P(),
    )
    out_specs = (P("row", "col"), P("row", "col"), P("row", "col", None))
    return jax.shard_map(shards, mesh=mesh, in_specs=in_specs, out_specs=out_specs, check_vma=False)
```
